32 devices in a mesh: top: 4 (over x, core), low: 8 (over z, y).
Axes of the slice: x: 2, y: 2, z: 4, core: 2. Of those that a mesh axis runs over, the one named last changes fastest.
Arguments:
- segments: float32 [8192, 9, 128], P(('top', 'low')), may hold values from -1 to 1
- send_counts: int32 [32, 32], P(('top', 'low')), may hold values from 0 to 16, as said below
- send_offsets: int32 [32, 32], P(('top', 'low')), may hold values from 0 to 256, as said below
- leaf_of_block: int32 [8192], P(('top', 'low')), may hold values from 0 to 127
Outputs:
- leaf_moments: float32 [315, 4096], P(None, ('top', 'low'))
- root_moments: float32 [32, 315], P(('top', 'low'))
The draws below stay inside these ranges and needn't reach their ends.
Inputs may be any that keep to these rules, and one draw needn't show every extreme that they name: `send_counts`: each row sums to 256; one owner, drawn from the seed, receives exactly 16 blocks from every domain. `send_offsets`: each row is the exclusive prefix sum of the same row of send_counts.
All inputs are finite; a program needn't handle non-finite values.
Results may differ from the reference program's by a relative error of at most 0.00017.
Values sent between devices are 32-bit elements; how exact they have to be, the bound alone decides.
A program may use at most 192 MiB of HBM per device.

```python
import math
import jax
import jax.numpy as jnp
import numpy as np
from jax import lax

SEG_BLOCK = 128
COEFFS = 315
BLK_DEV = 256
CAP = 16
LEAF_DEV = 128
BLOCKS = 8192
LEAVES = 4096
DEVICES = 32


def counts_helper(key):
    base_key = jax.random.fold_in(key, 7)
    heavy = jax.random.randint(jax.random.fold_in(base_key, 1), (), 0, DEVICES)
    remaining = BLK_DEV - CAP
    others = DEVICES - 1

    def one_row(row_key):
        shuffled = jax.random.permutation(row_key, others * CAP)
        picked = shuffled[:remaining] // CAP
        tallies = jnp.sum((picked[:, None] == jnp.arange(others)[None, :]).astype(jnp.int32), axis=0)
        owner_ids = jnp.arange(DEVICES)
        source_ids = jnp.clip(jnp.where(owner_ids < heavy, owner_ids, owner_ids - 1), 0, others - 1)
        return jnp.where(owner_ids == heavy, CAP, tallies[source_ids]).astype(jnp.int32)
    row_keys = jax.random.split(jax.random.fold_in(base_key, 2), DEVICES)
    return jax.vmap(one_row)(row_keys)


def draw_send_counts(key, part):
    return counts_helper(key)


def draw_send_offsets(key, part):
    tallies = counts_helper(key)
    return (jnp.cumsum(tallies, axis=1) - tallies).astype(jnp.int32)


def set_ends(result, own_key, smallest, largest):
    dims = result.shape
    spot = [jax.random.randint(jax.random.fold_in(own_key, axis), (), 0, dims[axis]) for axis in range(len(dims))]
    result = result.at[tuple(spot)].set(smallest)
    longest = dims.index(max(dims))
    spot[longest] = (spot[longest] + 1) % dims[longest]
    return result.at[tuple(spot)].set(largest)


def steps_of(stream_key, extent, cuts, low, largest):
    loudness = 1.0
    for dim, shards_of in cuts:
        steps = jax.random.uniform(jax.random.fold_in(jax.random.fold_in(stream_key, 6), dim), (shards_of,), jnp.float32, low / len(cuts), largest / len(cuts))
        loudness = loudness * jnp.repeat(jnp.exp(steps), extent[dim] // shards_of).reshape((-1,) + (1,) * (len(extent) - 1 - dim))
    return loudness


def setup_inputs(seed: int = 0) -> dict:
    streams_of = jax.random.split(jax.random.key(seed), 5)
    return {
        "segments": jnp.clip(jax.random.uniform(streams_of[0], (BLOCKS, 9, SEG_BLOCK), jnp.float32, -1.0, 1.0) * steps_of(streams_of[0], (BLOCKS, 9, SEG_BLOCK), ((0, 32),), -0.4, 0.0), -1.0, 1.0),
        "send_counts": draw_send_counts(jax.random.fold_in(streams_of[4], 71), 0),
        "send_offsets": draw_send_offsets(jax.random.fold_in(streams_of[4], 71), 0),
        "leaf_of_block": set_ends(jax.random.randint(streams_of[3], (BLOCKS,), 0, LEAF_DEV), jax.random.fold_in(streams_of[3], 1), 0, LEAF_DEV - 1).astype(jnp.int32),
    }


def make_exponents():
    collected = []
    for degree_total in range(5):
        for first_power in range(degree_total, -1, -1):
            for second_power in range(degree_total - first_power, -1, -1):
                collected.append((first_power, second_power, degree_total - first_power - second_power))
    return np.array(collected, dtype=np.int32)

def make_shifts(which_axis):
    exponent_table = make_exponents()
    table = np.zeros((2, 35, 35), np.float32)
    for which_side in range(2):
        sign_value = -1.0 if which_side == 0 else 1.0
        for target_row in range(35):
            for source_col in range(35):
                target = exponent_table[target_row]
                source = exponent_table[source_col]
                agrees = all((target[other] == source[other] for other in range(3) if other != which_axis))
                if agrees and source[which_axis] <= target[which_axis]:
                    upper_power = int(target[which_axis])
                    lower_power = int(source[which_axis])
                    table[which_side, target_row, source_col] = math.comb(upper_power, lower_power) * sign_value ** (upper_power - lower_power) * 0.5 ** upper_power
    return table

def quadrature():
    return ((-math.sqrt(0.6), 0.0, math.sqrt(0.6)), (5.0 / 18.0, 8.0 / 18.0, 5.0 / 18.0))

def block_moments(blocks):
    exponent_table = make_exponents()
    gauss_points, gauss_weights = quadrature()
    how_many = blocks.shape[0]
    seg_width = blocks.shape[2]
    burgers = blocks[:, 0:3]
    middle = blocks[:, 3:6]
    half_vector = blocks[:, 6:9]
    tensor = (burgers[:, :, None, :] * (2.0 * half_vector)[:, None, :, :]).reshape(how_many, 9, seg_width)
    monomials = jnp.zeros((how_many, 35, seg_width), jnp.float32)
    for gauss_point, weight in zip(gauss_points, gauss_weights):
        position = middle + gauss_point * half_vector
        squared = position * position
        powers = jnp.stack([jnp.ones_like(position), position, squared, squared * position, squared * squared], axis=1)
        monomials = monomials + weight * (powers[:, exponent_table[:, 0], 0] * powers[:, exponent_table[:, 1], 1] * powers[:, exponent_table[:, 2], 2])
    moments = jnp.einsum('bas,bms->bam', tensor, monomials, precision=lax.Precision.HIGHEST)
    return (moments * seg_width ** (-0.5)).reshape(how_many, 9 * 35)

def combine_level(lower, upper, which_dim):
    tables = jnp.asarray(make_shifts(which_dim))
    left_part = jnp.einsum('mk,akn->amn', tables[0], lower, precision=lax.Precision.HIGHEST)
    right_part = jnp.einsum('mk,akn->amn', tables[1], upper, precision=lax.Precision.HIGHEST)
    return (left_part + right_part) * (1.0 / math.sqrt(2.0))

def reduce_tree(cells, first_level):
    levels = cells.shape[2].bit_length() - 1
    for level_index in range(levels):
        paired = cells.reshape(9, 35, -1, 2)
        cells = combine_level(paired[..., 0], paired[..., 1], (first_level + level_index) % 3)
    return cells

def reference(segments, send_counts, send_offsets, leaf_of_block):
    range_ends = send_offsets + send_counts
    positions = jnp.arange(BLK_DEV, dtype=jnp.int32)
    owners = lax.optimization_barrier(jnp.sum((range_ends[:, None, :] <= positions[None, :, None]).astype(jnp.int32), axis=2))
    global_leaf = (owners.reshape(-1) * LEAF_DEV + leaf_of_block).astype(jnp.int32)
    grouped = segments.reshape(DEVICES, BLK_DEV, 9, SEG_BLOCK)
    moments = lax.map(block_moments, grouped).reshape(DEVICES * BLK_DEV, COEFFS)
    leaf_cells = jax.ops.segment_sum(moments, global_leaf, num_segments=LEAVES)
    leaf_moments = jnp.transpose(leaf_cells)
    root = reduce_tree(leaf_moments.reshape(9, 35, LEAVES), 0).reshape(1, COEFFS)
    return (leaf_moments, jnp.broadcast_to(root, (DEVICES, COEFFS)))
```

```python
import functools
import math

import jax
import jax.numpy as jnp
import numpy as np
from jax import lax
from jax.experimental import pallas as pl
from jax.experimental.pallas import tpu as pltpu
from jax.sharding import PartitionSpec as P

MONOS = 35
COEFFS = 315
LEAF_DEV = 128
SLOTS = 16
ROWS = 2 * SLOTS + SLOTS // 2
MESH = pl.DeviceIdType.MESH
BF16 = jnp.bfloat16
F32 = jnp.float32
NT = (((1,), (1,)), ((), ()))
NN = (((1,), (0,)), ((), ()))


def make_exponents():
    collected = []
    for degree_total in range(5):
        for first_power in range(degree_total, -1, -1):
            for second_power in range(degree_total - first_power, -1, -1):
                collected.append(
                    (first_power, second_power, degree_total - first_power - second_power)
                )
    return collected


EXPONENTS = make_exponents()
POINTS = (
    (-math.sqrt(0.6), 5.0 / 18.0),
    (0.0, 8.0 / 18.0),
    (math.sqrt(0.6), 5.0 / 18.0),
)


def make_permutation():
    table = np.zeros((320, 384), np.float32)
    for m in range(MONOS):
        for a in range(9):
            table[MONOS * a + m, 128 * (m // 14) + 9 * (m % 14) + a] = 1.0
    return table


def split(x):
    high = x.astype(BF16)
    low = (x - high.astype(F32)).astype(BF16)
    return high, low


def dot(a, b, dims):
    return lax.dot_general(a, b, dims, preferred_element_type=F32)


def monomials(middle, half):
    total = None
    for point, weight in POINTS:
        at = [m + point * h if point else m for m, h in zip(middle, half)]
        made = {(0, 0, 0): None}
        values = []
        for e in EXPONENTS[1:]:
            axis = next(i for i in range(3) if e[i] > 0)
            lower = tuple(p - (i == axis) for i, p in enumerate(e))
            before = made[lower]
            made[e] = at[axis] * weight if before is None else before * at[axis]
            values.append(made[e])
        total = values if total is None else [x + y for x, y in zip(total, values)]
    return [jnp.ones_like(middle[0])] + total


def pair_products(quads, tensors):
    q_high, q_low = split(jnp.concatenate(quads, axis=0))
    t_high, t_low = split(jnp.concatenate(tensors + [jnp.zeros((56, 128), F32)], axis=0))
    left = jnp.concatenate([q_high, q_low], axis=1)
    right = jnp.concatenate([t_high, t_low], axis=0)
    both = dot(left, jnp.concatenate([right, right], axis=1), NT)
    return both[:, :128] + both[:, 128:]


def gather_same(products, spread):
    rows = products.shape[0]
    lane = lax.broadcasted_iota(jnp.int32, (rows, 128), 1)
    row = lax.broadcasted_iota(jnp.int32, (rows, 128), 0)
    kept = jnp.where(lax.rem(lane, 8) == lax.rem(row, 8), products, 0.0)
    high, low = split(kept)
    spreaded = dot(jnp.concatenate([high, low], axis=1), spread, NN)
    lane8 = lax.broadcasted_iota(jnp.int32, (8, 128), 1)
    tiles = []
    for first in (0, 14, 28):
        tile = jnp.zeros((8, 128), F32)
        for k in range(min(14, MONOS - first)):
            m = first + k
            here = (lane8 >= 9 * k) & (lane8 < 9 * k + 9)
            tile = jnp.where(here, spreaded[8 * m : 8 * m + 8], tile)
        tiles.append(tile)
    return tiles


def column(row):
    return jnp.transpose(jnp.broadcast_to(row, (128, 128)))


def kernel(
    devices, low_size, seg_ref, leaf_ref, perm_ref, spread_ref, count_ref, offset_ref,
    leaf_out, root_out,
    place, moments, acc, sbuf, rbuf, root_send, root_recv,
    send_sem, recv_sem, root_send_sem, root_recv_sem,
):
    me = lax.axis_index("top") * low_size + lax.axis_index("low")
    blocks = seg_ref.shape[1]
    groups = blocks // 8

    def partner(step):
        other = lax.rem(me + step, devices)
        return other, (other // low_size, lax.rem(other, low_size))

    barrier = pltpu.get_barrier_semaphore()

    def greet(step, carry):
        pl.semaphore_signal(barrier, inc=1, device_id=partner(step)[1], device_id_type=MESH)
        return carry

    lax.fori_loop(1, devices, greet, 0)

    leaves = leaf_ref[...]
    for chunk in range(blocks // 128):
        place[3, chunk * 128 : chunk * 128 + 128] = column(
            leaves[chunk : chunk + 1].astype(F32)
        )

    def load(group):
        rows = pl.ds(pl.multiple_of(group * 8, 8), 8)
        parts = [seg_ref[c, rows, :] for c in range(9)]
        scaled = [h * (2.0 / math.sqrt(128.0)) for h in parts[6:9]]
        tensors = [b * h for b in parts[0:3] for h in scaled]
        return rows, parts[3:6], parts[6:9], tensors

    lane8 = lax.broadcasted_iota(jnp.int32, (8, 128), 1)

    def p2m(group, carry):
        rows, middle, half, tensors = load(group)
        products = pair_products(monomials(middle, half), tensors)
        first, second, third = gather_same(products, spread_ref[...])
        moments[0, rows, :] = first
        moments[1, rows, :] = second
        moments[2, rows, :] = jnp.where(lane8 == 63, place[3, rows, :], third)
        return carry

    lax.fori_loop(0, groups, p2m, 0, unroll=2)
    for tile in range(3):
        moments[tile, blocks : blocks + SLOTS, :] = jnp.zeros((SLOTS, 128), F32)

    pl.semaphore_wait(barrier, devices - 1)

    lane16 = lax.broadcasted_iota(jnp.int32, (SLOTS, 128), 1)
    slot16 = lax.broadcasted_iota(jnp.int32, (SLOTS, 128), 0)

    def packed(owner):
        rows = pl.ds(offset_ref[0, owner], SLOTS)
        dead = (lane16 == 63) & (slot16 >= count_ref[0, owner])
        third = jnp.where(dead, -1.0, moments[2, rows, :])
        folded = jnp.where(lane8 < 64, third[:8], pltpu.roll(third[8:], 64, 1))
        return moments[0, rows, :], moments[1, rows, :], folded

    def put(ref, step, pieces):
        ref[step, 0:SLOTS, :] = pieces[0]
        ref[step, SLOTS : 2 * SLOTS, :] = pieces[1]
        ref[step, 2 * SLOTS : ROWS, :] = pieces[2]

    def block_copy(step):
        return pltpu.make_async_remote_copy(
            src_ref=sbuf.at[step], dst_ref=rbuf.at[step],
            send_sem=send_sem.at[step], recv_sem=recv_sem.at[step],
            device_id=partner(step)[1], device_id_type=MESH,
        )

    def root_copy(step):
        return pltpu.make_async_remote_copy(
            src_ref=root_send, dst_ref=root_recv.at[step],
            send_sem=root_send_sem.at[step], recv_sem=root_recv_sem.at[step],
            device_id=partner(step)[1], device_id_type=MESH,
        )

    def send_blocks(step, carry):
        put(sbuf, step, packed(partner(step)[0]))
        block_copy(step).start()
        return carry

    lax.fori_loop(1, devices, send_blocks, 0)
    put(rbuf, 0, packed(me))

    levels = LEAF_DEV.bit_length() - 1 + devices.bit_length() - 1
    depth = [len(range(d, levels, 3)) for d in range(3)]
    for chunk in range(blocks // 128):
        index = lax.broadcasted_iota(jnp.int32, (1, 128), 1) + chunk * 128
        owner = jnp.zeros((1, 128), jnp.int32)
        for o in range(devices):
            end = offset_ref[0, o] + count_ref[0, o]
            owner = owner + jnp.where(index >= end, 1, 0)
        cell = owner * LEAF_DEV + leaves[chunk : chunk + 1]
        for d in range(3):
            centre = jnp.zeros((1, 128), F32)
            for level in range(d, levels, 3):
                bit = lax.shift_right_logical(cell, level) & 1
                centre = centre + jnp.where(bit == 1, 1.0, -1.0) * 2.0 ** (level // 3)
            place[d, chunk * 128 : chunk * 128 + 128] = column(centre)

    acc[...] = jnp.zeros_like(acc)

    def to_root(group, carry):
        rows, middle, half, tensors = load(group)
        shrink = [0.5**k for k in depth]
        middle = [(p + place[d, rows, :]) * shrink[d] for d, p in enumerate(middle)]
        half = [h * shrink[d] for d, h in enumerate(half)]
        acc[...] += pair_products(monomials(middle, half), tensors)
        return carry

    lax.fori_loop(0, groups, to_root, 0, unroll=2)
    tiles = gather_same(acc[...] * 2.0 ** (-levels / 2), spread_ref[...])
    own = jnp.concatenate(
        [jnp.sum(t, axis=0, keepdims=True) for t in tiles] + [jnp.zeros((5, 128), F32)], axis=0
    )
    root_send[...] = own

    def send_root(step, carry):
        root_copy(step).start()
        return carry

    lax.fori_loop(1, devices, send_root, 0)

    def take(step, carry):
        block_copy(step).wait()
        return carry

    lax.fori_loop(1, devices, take, 0)

    half_rows = devices * 8
    flat = lambda x: x.reshape(half_rows, 128)
    near = [flat(rbuf[:, 0:8]), flat(rbuf[:, 16:24]), flat(rbuf[:, 32:40])]
    far = [flat(rbuf[:, 8:16]), flat(rbuf[:, 24:32]), pltpu.roll(near[2], 64, 1)]
    leaf_lane = lax.broadcasted_iota(jnp.int32, (half_rows, 128), 1).astype(F32)
    cells = jnp.zeros((LEAF_DEV, 384), F32)
    for side in (near, far):
        hit = jnp.where(side[2][:, 63:64] == leaf_lane, 1.0, 0.0)
        hit = jnp.transpose(hit).astype(BF16)
        high, low = split(jnp.concatenate(side, axis=1))
        cells = cells + dot(hit, high, NN) + dot(hit, low, NN)
    perm = perm_ref[...]
    high, low = split(cells)
    leaf_out[...] = (dot(perm, high, NT) + dot(perm, low, NT))[:COEFFS]

    def take_root(step, carry):
        root_copy(step).wait()
        return carry

    lax.fori_loop(1, devices, take_root, 0)
    root_recv[0] = own
    total = jnp.sum(root_recv[...], axis=0)
    line = jnp.concatenate([total[0:1], total[1:2], total[2:3]], axis=1)
    high, low = split(jnp.broadcast_to(line, (16, 384)))
    root_out[...] = (dot(high, perm, NT) + dot(low, perm, NT))[0:1, :COEFFS]


def local(devices, low_size, segments, send_counts, send_offsets, leaf_of_block):
    blocks = segments.shape[0]
    lanes = np.arange(128)
    one = ((lanes[None, :] % 9 == lanes[:, None] // 8) & (lanes[:, None] < 72)).astype(np.float32)
    spread = jnp.asarray(np.concatenate([one, one], axis=0), BF16)
    perm = jnp.asarray(make_permutation(), BF16)
    vmem = pl.BlockSpec(memory_space=pltpu.VMEM)
    smem = pl.BlockSpec(memory_space=pltpu.SMEM)
    dma = pltpu.SemaphoreType.DMA
    return pl.pallas_call(
        functools.partial(kernel, devices, low_size),
        out_shape=(
            jax.ShapeDtypeStruct((COEFFS, LEAF_DEV), F32),
            jax.ShapeDtypeStruct((1, COEFFS), F32),
        ),
        in_specs=[vmem, vmem, vmem, vmem, smem, smem],
        out_specs=(vmem, vmem),
        scratch_shapes=[
            pltpu.VMEM((4, blocks, 128), F32),
            pltpu.VMEM((3, blocks + SLOTS, 128), F32),
            pltpu.VMEM((8 * MONOS, 128), F32),
            pltpu.VMEM((devices, ROWS, 128), F32),
            pltpu.VMEM((devices, ROWS, 128), F32),
            pltpu.VMEM((8, 128), F32),
            pltpu.VMEM((devices, 8, 128), F32),
            dma((devices,)),
            dma((devices,)),
            dma((devices,)),
            dma((devices,)),
        ],
        compiler_params=pltpu.CompilerParams(
            collective_id=0, has_side_effects=True, vmem_limit_bytes=40 * 1024 * 1024
        ),
        cost_estimate=pl.CostEstimate(
            flops=2 * blocks * 128 * COEFFS * 2, bytes_accessed=blocks * 128 * 40, transcendentals=0
        ),
    )(
        jnp.transpose(segments, (1, 0, 2)),
        leaf_of_block.reshape(blocks // 128, 128),
        perm,
        spread,
        send_counts,
        send_offsets,
    )


def solution(mesh):
    placed = (
        P(("top", "low"), None, None),
        P(("top", "low"), None),
        P(("top", "low"), None),
        P(("top", "low")),
    )
    return jax.shard_map(
        functools.partial(local, mesh.size, mesh.shape["low"]),
        mesh=mesh,
        in_specs=placed,
        out_specs=(P(None, ("top", "low")), P(("top", "low"), None)),
        check_vma=False,
    )
```

```python
import functools
import math

import jax
import jax.numpy as jnp
import numpy as np
from jax import lax
from jax.experimental import pallas as pl
from jax.experimental.pallas import tpu as pltpu
from jax.sharding import PartitionSpec as P

MONOS = 35
COEFFS = 315
LEAF_DEV = 128
SLOTS = 16
ROWS = 2 * SLOTS + SLOTS // 2
TOGETHER = 4
MESH = pl.DeviceIdType.MESH
BF16 = jnp.bfloat16
F32 = jnp.float32
NT = (((1,), (1,)), ((), ()))
NN = (((1,), (0,)), ((), ()))


def make_exponents():
    collected = []
    for degree_total in range(5):
        for first_power in range(degree_total, -1, -1):
            for second_power in range(degree_total - first_power, -1, -1):
                collected.append(
                    (first_power, second_power, degree_total - first_power - second_power)
                )
    return collected


EXPONENTS = make_exponents()
POINTS = (
    (-math.sqrt(0.6), 5.0 / 18.0),
    (0.0, 8.0 / 18.0),
    (math.sqrt(0.6), 5.0 / 18.0),
)


def make_permutation():
    table = np.zeros((320, 384), np.float32)
    for m in range(MONOS):
        for a in range(9):
            table[MONOS * a + m, 128 * (m // 14) + 9 * (m % 14) + a] = 1.0
    return table


def split(x):
    high = x.astype(BF16)
    low = (x - high.astype(F32)).astype(BF16)
    return high, low


def dot(a, b, dims):
    return lax.dot_general(a, b, dims, preferred_element_type=F32)


def monomials(middle, half):
    total = None
    for point, weight in POINTS:
        at = [m + point * h if point else m for m, h in zip(middle, half)]
        made = {(0, 0, 0): None}
        values = []
        for e in EXPONENTS[1:]:
            axis = next(i for i in range(3) if e[i] > 0)
            lower = tuple(p - (i == axis) for i, p in enumerate(e))
            before = made[lower]
            made[e] = at[axis] * weight if before is None else before * at[axis]
            values.append(made[e])
        total = values if total is None else [x + y for x, y in zip(total, values)]
    return [jnp.ones_like(middle[0])] + total


def pair_products(quads, tensors):
    q_high, q_low = split(jnp.concatenate(quads, axis=0))
    t_high, t_low = split(jnp.concatenate(tensors + [jnp.zeros((56, 128), F32)], axis=0))
    left = jnp.concatenate([q_high, q_low], axis=1)
    right = jnp.concatenate([t_high, t_low], axis=0)
    both = dot(left, jnp.concatenate([right, right], axis=1), NT)
    return both[:, :128] + both[:, 128:]


def gather_same(products, same, spread, lane):
    sides = []
    for one in products:
        kept = (one.reshape(MONOS, 8, 128) * same).reshape(8 * MONOS, 128)
        sides.append(jnp.concatenate(split(kept), axis=1))
    spreaded = dot(jnp.concatenate(sides, axis=0), spread, NN)
    groups = []
    for g in range(len(products)):
        tiles = []
        for first in (0, 14, 28):
            count = min(14, MONOS - first)
            tile = jnp.zeros((8, 128), F32)
            for k in reversed(range(count)):
                at = 8 * (MONOS * g + first + k)
                tile = jnp.where(lane < 9 * k + 9, spreaded[at : at + 8], tile)
            tiles.append(tile)
        groups.append(tiles)
    return groups


def column(row):
    return jnp.transpose(jnp.broadcast_to(row, (128, 128)))


def kernel(
    devices, low_size, cap,
    seg_hbm, leaf_hbm, perm_hbm, spread_hbm, count_hbm, offset_hbm,
    leaf_out, root_out,
    seg_ref, leaf_ref, perm_ref, spread_ref, count_ref, offset_ref,
    place, moments, acc, sbuf, rbuf, root_send, root_recv,
    load_sem, send_sem, recv_sem, root_send_sem, root_recv_sem,
):
    fetches = [
        pltpu.make_async_copy(src, dst, load_sem.at[i])
        for i, (src, dst) in enumerate(
            (
                (leaf_hbm, leaf_ref),
                (seg_hbm, seg_ref),
                (spread_hbm, spread_ref),
                (count_hbm, count_ref),
                (offset_hbm, offset_ref),
                (perm_hbm, perm_ref),
            )
        )
    ]
    for fetch in fetches:
        fetch.start()

    me = lax.axis_index("top") * low_size + lax.axis_index("low")
    blocks = seg_ref.shape[1]

    def partner(step):
        other = lax.rem(me + step, devices)
        return other, (other // low_size, lax.rem(other, low_size))

    barrier = pltpu.get_barrier_semaphore()

    def greet(step, carry):
        pl.semaphore_signal(barrier, inc=1, device_id=partner(step)[1], device_id_type=MESH)
        return carry

    lax.fori_loop(1, devices, greet, 0)
    moments[...] = jnp.zeros_like(moments)
    acc[...] = jnp.zeros_like(acc)

    fetches[0].wait()
    leaves = leaf_ref[...]
    for chunk in range(blocks // 128):
        place[3, chunk * 128 : chunk * 128 + 128] = column(
            leaves[chunk : chunk + 1].astype(F32)
        )
    for fetch in fetches[1:5]:
        fetch.wait()

    lane8 = lax.broadcasted_iota(jnp.int32, (8, 128), 1)
    row8 = lax.broadcasted_iota(jnp.int32, (8, 128), 0)
    same = jnp.where(lax.rem(lane8, 8) == row8, 1.0, 0.0)

    def load(group):
        rows = pl.ds(pl.multiple_of(group * 8, 8), 8)
        parts = [seg_ref[c, rows, :] for c in range(9)]
        scaled = [h * (2.0 / math.sqrt(128.0)) for h in parts[6:9]]
        tensors = [b * h for b in parts[0:3] for h in scaled]
        return rows, parts[3:6], parts[6:9], tensors

    def p2m(first_group):
        def body(turn, carry):
            products, places = [], []
            for u in range(TOGETHER):
                rows, middle, half, tensors = load(first_group + turn * TOGETHER + u)
                products.append(pair_products(monomials(middle, half), tensors))
                places.append(rows)
            for rows, tiles in zip(places, gather_same(products, same, spread_ref[...], lane8)):
                moments[0, rows, :] = tiles[0]
                moments[1, rows, :] = tiles[1]
                moments[2, rows, :] = jnp.where(lane8 == 63, place[3, rows, :], tiles[2])
            return carry

        return body

    lane16 = lax.broadcasted_iota(jnp.int32, (SLOTS, 128), 1)
    slot16 = lax.broadcasted_iota(jnp.int32, (SLOTS, 128), 0)

    def packed(owner):
        rows = pl.ds(offset_ref[0, owner], SLOTS)
        dead = (lane16 == 63) & (slot16 >= count_ref[0, owner])
        third = jnp.where(dead, -1.0, moments[2, rows, :])
        folded = jnp.where(lane8 < 64, third[:8], pltpu.roll(third[8:], 64, 1))
        return moments[0, rows, :], moments[1, rows, :], folded

    def put(ref, step, pieces):
        ref[step, 0:SLOTS, :] = pieces[0]
        ref[step, SLOTS : 2 * SLOTS, :] = pieces[1]
        ref[step, 2 * SLOTS : ROWS, :] = pieces[2]

    def block_copy(step):
        return pltpu.make_async_remote_copy(
            src_ref=sbuf.at[step], dst_ref=rbuf.at[step],
            send_sem=send_sem.at[step], recv_sem=recv_sem.at[step],
            device_id=partner(step)[1], device_id_type=MESH,
        )

    def root_copy(step):
        return pltpu.make_async_remote_copy(
            src_ref=root_send, dst_ref=root_recv.at[step],
            send_sem=root_send_sem.at[step], recv_sem=root_recv_sem.at[step],
            device_id=partner(step)[1], device_id_type=MESH,
        )

    quarter = blocks // 4
    ready = quarter // cap
    turns = quarter // (8 * TOGETHER)
    lax.fori_loop(0, turns, p2m(0), 0)
    lax.fori_loop(0, turns, p2m(3 * quarter // 8), 0)
    pl.semaphore_wait(barrier, devices - 1)

    def send_early(turn, carry):
        spot = lax.rem(me + turn, 2 * ready)
        owner = jnp.where(spot < ready, spot, devices - 2 * ready + spot)
        step = lax.rem(owner - me + devices, devices)

        @pl.when(step != 0)
        def _():
            put(sbuf, step, packed(owner))
            block_copy(step).start()

        return carry

    lax.fori_loop(0, 2 * ready, send_early, 0)
    lax.fori_loop(0, 2 * turns, p2m(quarter // 8), 0)

    def send_late(step, carry):
        owner = partner(step)[0]

        @pl.when((owner >= ready) & (owner < devices - ready))
        def _():
            put(sbuf, step, packed(owner))
            block_copy(step).start()

        return carry

    lax.fori_loop(1, devices, send_late, 0)
    put(rbuf, 0, packed(me))

    levels = LEAF_DEV.bit_length() - 1 + devices.bit_length() - 1
    depth = [len(range(d, levels, 3)) for d in range(3)]
    for chunk in range(blocks // 128):
        index = lax.broadcasted_iota(jnp.int32, (1, 128), 1) + chunk * 128
        owner = jnp.zeros((1, 128), jnp.int32)
        for o in range(devices):
            end = offset_ref[0, o] + count_ref[0, o]
            owner = owner + jnp.where(index >= end, 1, 0)
        cell = owner * LEAF_DEV + leaves[chunk : chunk + 1]
        for d in range(3):
            centre = jnp.zeros((1, 128), F32)
            for level in range(d, levels, 3):
                bit = lax.shift_right_logical(cell, level) & 1
                centre = centre + jnp.where(bit == 1, 1.0, -1.0) * 2.0 ** (level // 3)
            place[d, chunk * 128 : chunk * 128 + 128] = column(centre)

    def to_root(turn, carry):
        shrink = [0.5**k for k in depth]
        total = None
        for u in range(2):
            rows, middle, half, tensors = load(turn * 2 + u)
            middle = [(p + place[d, rows, :]) * shrink[d] for d, p in enumerate(middle)]
            half = [h * shrink[d] for d, h in enumerate(half)]
            products = pair_products(monomials(middle, half), tensors)
            total = products if total is None else total + products
        acc[...] += total
        return carry

    lax.fori_loop(0, blocks // 16, to_root, 0)
    (tiles,) = gather_same([acc[...] * 2.0 ** (-levels / 2)], same, spread_ref[...], lane8)
    own = jnp.concatenate(
        [jnp.sum(t, axis=0, keepdims=True) for t in tiles] + [jnp.zeros((5, 128), F32)], axis=0
    )
    root_send[...] = own

    def send_root(step, carry):
        root_copy(step).start()
        return carry

    lax.fori_loop(1, devices, send_root, 0)

    def take(step, carry):
        block_copy(step).wait()
        return carry

    part = devices // 2
    half_rows = part * 8
    flat = lambda x: x.reshape(half_rows, 128)
    leaf_lane = lax.broadcasted_iota(jnp.int32, (half_rows, 128), 1).astype(F32)
    cells = jnp.zeros((LEAF_DEV, 384), F32)
    for start in (0, part):
        lax.fori_loop(max(start, 1), start + part, take, 0)
        got = pl.ds(start, part)
        near = [flat(rbuf[got, 0:8]), flat(rbuf[got, 16:24]), flat(rbuf[got, 32:40])]
        far = [flat(rbuf[got, 8:16]), flat(rbuf[got, 24:32]), pltpu.roll(near[2], 64, 1)]
        for side in (near, far):
            hit = jnp.where(side[2][:, 63:64] == leaf_lane, 1.0, 0.0)
            hit = jnp.transpose(hit).astype(BF16)
            high, low = split(jnp.concatenate(side, axis=1))
            cells = cells + dot(hit, high, NN) + dot(hit, low, NN)
    fetches[5].wait()
    perm = perm_ref[...]
    high, low = split(cells)
    leaf_out[...] = (dot(perm, high, NT) + dot(perm, low, NT))[:COEFFS]

    def take_root(step, carry):
        root_copy(step).wait()
        return carry

    lax.fori_loop(1, devices, take_root, 0)
    root_recv[0] = own
    total = jnp.sum(root_recv[...], axis=0)
    line = jnp.concatenate([total[0:1], total[1:2], total[2:3]], axis=1)
    high, low = split(jnp.broadcast_to(line, (16, 384)))
    root_out[...] = (dot(high, perm, NT) + dot(low, perm, NT))[0:1, :COEFFS]


def local(devices, low_size, segments, send_counts, send_offsets, leaf_of_block):
    blocks = segments.shape[0]
    lanes = np.arange(128)
    one = ((lanes[None, :] % 9 == lanes[:, None] // 8) & (lanes[:, None] < 72)).astype(np.float32)
    spread = jnp.asarray(np.concatenate([one, one], axis=0), BF16)
    perm = jnp.asarray(make_permutation(), BF16)
    vmem = pl.BlockSpec(memory_space=pltpu.VMEM)
    hbm = pl.BlockSpec(memory_space=pltpu.HBM)
    cap = max(2, 2 * blocks // devices)
    dma = pltpu.SemaphoreType.DMA
    return pl.pallas_call(
        functools.partial(kernel, devices, low_size, cap),
        out_shape=(
            jax.ShapeDtypeStruct((COEFFS, LEAF_DEV), F32),
            jax.ShapeDtypeStruct((1, COEFFS), F32),
        ),
        in_specs=[hbm] * 6,
        out_specs=(vmem, vmem),
        scratch_shapes=[
            pltpu.VMEM((9, blocks, 128), F32),
            pltpu.VMEM((blocks // 128, 128), jnp.int32),
            pltpu.VMEM((320, 384), BF16),
            pltpu.VMEM((256, 128), BF16),
            pltpu.SMEM((1, devices), jnp.int32),
            pltpu.SMEM((1, devices), jnp.int32),
            pltpu.VMEM((4, blocks, 128), F32),
            pltpu.VMEM((3, blocks + SLOTS, 128), F32),
            pltpu.VMEM((8 * MONOS, 128), F32),
            pltpu.VMEM((devices, ROWS, 128), F32),
            pltpu.VMEM((devices, ROWS, 128), F32),
            pltpu.VMEM((8, 128), F32),
            pltpu.VMEM((devices, 8, 128), F32),
            dma((6,)),
            dma((devices,)),
            dma((devices,)),
            dma((devices,)),
            dma((devices,)),
        ],
        compiler_params=pltpu.CompilerParams(
            collective_id=0, has_side_effects=True, vmem_limit_bytes=40 * 1024 * 1024
        ),
        cost_estimate=pl.CostEstimate(
            flops=2 * blocks * 128 * COEFFS * 2, bytes_accessed=blocks * 128 * 40, transcendentals=0
        ),
    )(
        jnp.transpose(segments, (1, 0, 2)),
        leaf_of_block.reshape(blocks // 128, 128),
        perm,
        spread,
        send_counts,
        send_offsets,
    )


def solution(mesh):
    placed = (
        P(("top", "low"), None, None),
        P(("top", "low"), None),
        P(("top", "low"), None),
        P(("top", "low")),
    )
    return jax.shard_map(
        functools.partial(local, mesh.size, mesh.shape["low"]),
        mesh=mesh,
        in_specs=placed,
        out_specs=(P(None, ("top", "low")), P(("top", "low"), None)),
        check_vma=False,
    )
```

```python
import functools
import math

import jax
import jax.numpy as jnp
import numpy as np
from jax import lax
from jax.experimental import pallas as pl
from jax.experimental.pallas import tpu as pltpu
from jax.sharding import PartitionSpec as P

MONOS = 35
COEFFS = 315
LEAF_DEV = 128
SLOTS = 16
ROWS = 2 * SLOTS + SLOTS // 2
TOGETHER = 4
MESH = pl.DeviceIdType.MESH
BF16 = jnp.bfloat16
F32 = jnp.float32
NT = (((1,), (1,)), ((), ()))
NN = (((1,), (0,)), ((), ()))


def make_exponents():
    collected = []
    for degree_total in range(5):
        for first_power in range(degree_total, -1, -1):
            for second_power in range(degree_total - first_power, -1, -1):
                collected.append(
                    (first_power, second_power, degree_total - first_power - second_power)
                )
    return collected


EXPONENTS = make_exponents()
POINTS = (
    (-math.sqrt(0.6), 5.0 / 18.0),
    (0.0, 8.0 / 18.0),
    (math.sqrt(0.6), 5.0 / 18.0),
)


def make_permutation():
    table = np.zeros((320, 384), np.float32)
    for m in range(MONOS):
        for a in range(9):
            table[MONOS * a + m, 128 * (m // 14) + 9 * (m % 14) + a] = 1.0
    return table


def split(x):
    high = x.astype(BF16)
    low = (x - high.astype(F32)).astype(BF16)
    return high, low


def dot(a, b, dims):
    return lax.dot_general(a, b, dims, preferred_element_type=F32)


def monomials(middle, half):
    total = None
    for point, weight in POINTS:
        at = [m + point * h if point else m for m, h in zip(middle, half)]
        made = {(0, 0, 0): None}
        values = []
        for e in EXPONENTS[1:]:
            axis = next(i for i in range(3) if e[i] > 0)
            lower = tuple(p - (i == axis) for i, p in enumerate(e))
            before = made[lower]
            made[e] = at[axis] * weight if before is None else before * at[axis]
            values.append(made[e])
        total = values if total is None else [x + y for x, y in zip(total, values)]
    return [jnp.ones_like(middle[0])] + total


def pair_products(quads, tensors):
    q_high, q_low = split(jnp.concatenate(quads, axis=0))
    t_high, t_low = split(jnp.concatenate(tensors + [jnp.zeros((56, 128), F32)], axis=0))
    left = jnp.concatenate([q_high, q_low], axis=1)
    right = jnp.concatenate([t_high, t_low], axis=0)
    both = dot(left, jnp.concatenate([right, right], axis=1), NT)
    return both[:, :128] + both[:, 128:]


def gather_same(products, same, spread, lane):
    sides = []
    for one in products:
        kept = (one.reshape(MONOS, 8, 128) * same).reshape(8 * MONOS, 128)
        sides.append(jnp.concatenate(split(kept), axis=1))
    spreaded = dot(jnp.concatenate(sides, axis=0), spread, NN)
    groups = []
    for g in range(len(products)):
        tiles = []
        for first in (0, 14, 28):
            count = min(14, MONOS - first)
            tile = jnp.zeros((8, 128), F32)
            for k in reversed(range(count)):
                at = 8 * (MONOS * g + first + k)
                tile = jnp.where(lane < 9 * k + 9, spreaded[at : at + 8], tile)
            tiles.append(tile)
        groups.append(tiles)
    return groups


def column(row):
    return jnp.transpose(jnp.broadcast_to(row, (128, 128)))


def kernel(
    devices, low_size, cap,
    seg_hbm, leaf_hbm, perm_hbm, spread_hbm, count_hbm, offset_hbm,
    leaf_out, root_out,
    seg_ref, leaf_ref, perm_ref, spread_ref, count_ref, offset_ref,
    place, moments, acc, sbuf, rbuf, root_send, root_recv,
    load_sem, send_sem, recv_sem, root_send_sem, root_recv_sem,
):
    fetches = [
        pltpu.make_async_copy(src, dst, load_sem.at[i])
        for i, (src, dst) in enumerate(
            (
                (leaf_hbm, leaf_ref),
                (seg_hbm, seg_ref),
                (spread_hbm, spread_ref),
                (count_hbm, count_ref),
                (offset_hbm, offset_ref),
                (perm_hbm, perm_ref),
            )
        )
    ]
    for fetch in fetches:
        fetch.start()

    me = lax.axis_index("top") * low_size + lax.axis_index("low")
    blocks = seg_ref.shape[1]

    def partner(step):
        other = lax.rem(me + step, devices)
        return other, (other // low_size, lax.rem(other, low_size))

    barrier = pltpu.get_barrier_semaphore()

    def greet(step, carry):
        pl.semaphore_signal(barrier, inc=1, device_id=partner(step)[1], device_id_type=MESH)
        return carry

    lax.fori_loop(1, devices, greet, 0)
    moments[...] = jnp.zeros_like(moments)
    acc[...] = jnp.zeros_like(acc)

    fetches[0].wait()
    leaves = leaf_ref[...]
    for chunk in range(blocks // 128):
        place[3, chunk * 128 : chunk * 128 + 128] = column(
            leaves[chunk : chunk + 1].astype(F32)
        )
    for fetch in fetches[1:5]:
        fetch.wait()

    lane8 = lax.broadcasted_iota(jnp.int32, (8, 128), 1)
    row8 = lax.broadcasted_iota(jnp.int32, (8, 128), 0)
    same = jnp.where(lax.rem(lane8, 8) == row8, 1.0, 0.0)

    def load(group):
        rows = pl.ds(pl.multiple_of(group * 8, 8), 8)
        parts = [seg_ref[c, rows, :] for c in range(9)]
        scaled = [h * (2.0 / math.sqrt(128.0)) for h in parts[6:9]]
        tensors = [b * h for b in parts[0:3] for h in scaled]
        return rows, parts[3:6], parts[6:9], tensors

    def p2m(first_group):
        def body(turn, carry):
            products, places = [], []
            for u in range(TOGETHER):
                rows, middle, half, tensors = load(first_group + turn * TOGETHER + u)
                products.append(pair_products(monomials(middle, half), tensors))
                places.append(rows)
            for rows, tiles in zip(places, gather_same(products, same, spread_ref[...], lane8)):
                moments[0, rows, :] = tiles[0]
                moments[1, rows, :] = tiles[1]
                moments[2, rows, :] = jnp.where(lane8 == 63, place[3, rows, :], tiles[2])
            return carry

        return body

    lane16 = lax.broadcasted_iota(jnp.int32, (SLOTS, 128), 1)
    slot16 = lax.broadcasted_iota(jnp.int32, (SLOTS, 128), 0)

    def packed(owner):
        rows = pl.ds(offset_ref[0, owner], SLOTS)
        dead = (lane16 == 63) & (slot16 >= count_ref[0, owner])
        third = jnp.where(dead, -1.0, moments[2, rows, :])
        folded = jnp.where(lane8 < 64, third[:8], pltpu.roll(third[8:], 64, 1))
        return moments[0, rows, :], moments[1, rows, :], folded

    def put(ref, step, pieces):
        ref[step, 0:SLOTS, :] = pieces[0]
        ref[step, SLOTS : 2 * SLOTS, :] = pieces[1]
        ref[step, 2 * SLOTS : ROWS, :] = pieces[2]

    def block_copy(step):
        return pltpu.make_async_remote_copy(
            src_ref=sbuf.at[step], dst_ref=rbuf.at[step],
            send_sem=send_sem.at[step], recv_sem=recv_sem.at[step],
            device_id=partner(step)[1], device_id_type=MESH,
        )

    def root_copy(step):
        return pltpu.make_async_remote_copy(
            src_ref=root_send, dst_ref=root_recv.at[step],
            send_sem=root_send_sem.at[step], recv_sem=root_recv_sem.at[step],
            device_id=partner(step)[1], device_id_type=MESH,
        )

    quarter = blocks // 4
    ready = quarter // cap
    turns = quarter // (8 * TOGETHER)
    lax.fori_loop(0, turns, p2m(0), 0)
    lax.fori_loop(0, turns, p2m(3 * quarter // 8), 0)
    pl.semaphore_wait(barrier, devices - 1)

    def send_early(turn, carry):
        spot = lax.rem(me + turn, 2 * ready)
        owner = jnp.where(spot < ready, spot, devices - 2 * ready + spot)
        step = lax.rem(owner - me + devices, devices)

        @pl.when(step != 0)
        def _():
            put(sbuf, step, packed(owner))
            block_copy(step).start()

        return carry

    lax.fori_loop(0, 2 * ready, send_early, 0)
    lax.fori_loop(0, 2 * turns, p2m(quarter // 8), 0)

    def send_late(step, carry):
        owner = partner(step)[0]

        @pl.when((owner >= ready) & (owner < devices - ready))
        def _():
            put(sbuf, step, packed(owner))
            block_copy(step).start()

        return carry

    lax.fori_loop(1, devices, send_late, 0)
    put(rbuf, 0, packed(me))

    levels = LEAF_DEV.bit_length() - 1 + devices.bit_length() - 1
    depth = [len(range(d, levels, 3)) for d in range(3)]
    for chunk in range(blocks // 128):
        index = lax.broadcasted_iota(jnp.int32, (1, 128), 1) + chunk * 128
        owner = jnp.zeros((1, 128), jnp.int32)
        for o in range(devices):
            end = offset_ref[0, o] + count_ref[0, o]
            owner = owner + jnp.where(index >= end, 1, 0)
        cell = owner * LEAF_DEV + leaves[chunk : chunk + 1]
        for d in range(3):
            centre = jnp.zeros((1, 128), F32)
            for level in range(d, levels, 3):
                bit = lax.shift_right_logical(cell, level) & 1
                centre = centre + jnp.where(bit == 1, 1.0, -1.0) * 2.0 ** (level // 3)
            place[d, chunk * 128 : chunk * 128 + 128] = column(centre)

    def to_root(turn, carry):
        shrink = [0.5**k for k in depth]
        total = None
        for u in range(2):
            rows, middle, half, tensors = load(turn * 2 + u)
            middle = [(p + place[d, rows, :]) * shrink[d] for d, p in enumerate(middle)]
            half = [h * shrink[d] for d, h in enumerate(half)]
            products = pair_products(monomials(middle, half), tensors)
            total = products if total is None else total + products
        acc[...] += total
        return carry

    lax.fori_loop(0, blocks // 16, to_root, 0)
    (tiles,) = gather_same([acc[...] * 2.0 ** (-levels / 2)], same, spread_ref[...], lane8)
    own = jnp.concatenate(
        [jnp.sum(t, axis=0, keepdims=True) for t in tiles] + [jnp.zeros((1, 128), F32)], axis=0
    )
    root_send[...] = own

    def send_root(step, carry):
        root_copy(step).start()
        return carry

    lax.fori_loop(1, devices, send_root, 0)

    def take(step, carry):
        block_copy(step).wait()
        return carry

    part = devices // 2
    half_rows = part * 8
    flat = lambda x: x.reshape(half_rows, 128)
    leaf_lane = lax.broadcasted_iota(jnp.int32, (half_rows, 128), 1).astype(F32)
    cells = jnp.zeros((LEAF_DEV, 384), F32)
    for start in (0, part):
        lax.fori_loop(max(start, 1), start + part, take, 0)
        got = pl.ds(start, part)
        near = [flat(rbuf[got, 0:8]), flat(rbuf[got, 16:24]), flat(rbuf[got, 32:40])]
        far = [flat(rbuf[got, 8:16]), flat(rbuf[got, 24:32]), pltpu.roll(near[2], 64, 1)]
        for side in (near, far):
            hit = jnp.where(side[2][:, 63:64] == leaf_lane, 1.0, 0.0)
            hit = jnp.transpose(hit).astype(BF16)
            high, low = split(jnp.concatenate(side, axis=1))
            cells = cells + dot(hit, high, NN) + dot(hit, low, NN)
    fetches[5].wait()
    perm = perm_ref[...]
    high, low = split(cells)
    leaf_out[...] = (dot(perm, high, NT) + dot(perm, low, NT))[:COEFFS]

    def take_root(step, carry):
        root_copy(step).wait()
        return carry

    lax.fori_loop(1, devices, take_root, 0)
    root_recv[0] = own
    total = jnp.sum(root_recv[...], axis=0)
    line = jnp.concatenate([total[0:1], total[1:2], total[2:3]], axis=1)
    high, low = split(jnp.broadcast_to(line, (16, 384)))
    root_out[...] = (dot(high, perm, NT) + dot(low, perm, NT))[0:1, :COEFFS]


def local(devices, low_size, segments, send_counts, send_offsets, leaf_of_block):
    blocks = segments.shape[0]
    lanes = np.arange(128)
    one = ((lanes[None, :] % 9 == lanes[:, None] // 8) & (lanes[:, None] < 72)).astype(np.float32)
    spread = jnp.asarray(np.concatenate([one, one], axis=0), BF16)
    perm = jnp.asarray(make_permutation(), BF16)
    vmem = pl.BlockSpec(memory_space=pltpu.VMEM)
    hbm = pl.BlockSpec(memory_space=pltpu.HBM)
    cap = max(2, 2 * blocks // devices)
    dma = pltpu.SemaphoreType.DMA
    return pl.pallas_call(
        functools.partial(kernel, devices, low_size, cap),
        out_shape=(
            jax.ShapeDtypeStruct((COEFFS, LEAF_DEV), F32),
            jax.ShapeDtypeStruct((1, COEFFS), F32),
        ),
        in_specs=[hbm] * 6,
        out_specs=(vmem, vmem),
        scratch_shapes=[
            pltpu.VMEM((9, blocks, 128), F32),
            pltpu.VMEM((blocks // 128, 128), jnp.int32),
            pltpu.VMEM((320, 384), BF16),
            pltpu.VMEM((256, 128), BF16),
            pltpu.SMEM((1, devices), jnp.int32),
            pltpu.SMEM((1, devices), jnp.int32),
            pltpu.VMEM((4, blocks, 128), F32),
            pltpu.VMEM((3, blocks + SLOTS, 128), F32),
            pltpu.VMEM((8 * MONOS, 128), F32),
            pltpu.VMEM((devices, ROWS, 128), F32),
            pltpu.VMEM((devices, ROWS, 128), F32),
            pltpu.VMEM((4, 128), F32),
            pltpu.VMEM((devices, 4, 128), F32),
            dma((6,)),
            dma((devices,)),
            dma((devices,)),
            dma((devices,)),
            dma((devices,)),
        ],
        compiler_params=pltpu.CompilerParams(
            collective_id=0, has_side_effects=True, vmem_limit_bytes=63 * 1024 * 1024
        ),
        cost_estimate=pl.CostEstimate(
            flops=2 * blocks * 128 * COEFFS * 2, bytes_accessed=blocks * 128 * 40, transcendentals=0
        ),
    )(
        jnp.transpose(segments, (1, 0, 2)),
        leaf_of_block.reshape(blocks // 128, 128),
        perm,
        spread,
        send_counts,
        send_offsets,
    )


def solution(mesh):
    placed = (
        P(("top", "low"), None, None),
        P(("top", "low"), None),
        P(("top", "low"), None),
        P(("top", "low")),
    )
    return jax.shard_map(
        functools.partial(local, mesh.size, mesh.shape["low"]),
        mesh=mesh,
        in_specs=placed,
        out_specs=(P(None, ("top", "low")), P(("top", "low"), None)),
        check_vma=False,
    )
```

```python
import functools
import math

import jax
import jax.numpy as jnp
import numpy as np
from jax import lax
from jax.experimental import pallas as pl
from jax.experimental.pallas import tpu as pltpu
from jax.sharding import PartitionSpec as P

MONOS = 35
COEFFS = 315
LEAF_DEV = 128
SLOTS = 16
ROWS = 2 * SLOTS + SLOTS // 2
TOGETHER = 4
MESH = pl.DeviceIdType.MESH
BF16 = jnp.bfloat16
F32 = jnp.float32
NT = (((1,), (1,)), ((), ()))
NN = (((1,), (0,)), ((), ()))


def make_exponents():
    collected = []
    for degree_total in range(5):
        for first_power in range(degree_total, -1, -1):
            for second_power in range(degree_total - first_power, -1, -1):
                collected.append(
                    (first_power, second_power, degree_total - first_power - second_power)
                )
    return collected


EXPONENTS = make_exponents()
POINTS = (
    (-math.sqrt(0.6), 5.0 / 18.0),
    (0.0, 8.0 / 18.0),
    (math.sqrt(0.6), 5.0 / 18.0),
)


def make_permutation():
    table = np.zeros((320, 384), np.float32)
    for m in range(MONOS):
        for a in range(9):
            table[MONOS * a + m, 128 * (m // 14) + 9 * (m % 14) + a] = 1.0
    return table


def split(x):
    high = x.astype(BF16)
    low = (x - high.astype(F32)).astype(BF16)
    return high, low


def dot(a, b, dims):
    return lax.dot_general(a, b, dims, preferred_element_type=F32)


def monomials(middle, half):
    total = None
    for point, weight in POINTS:
        at = [m + point * h if point else m for m, h in zip(middle, half)]
        made = {(0, 0, 0): None}
        values = []
        for e in EXPONENTS[1:]:
            axis = next(i for i in range(3) if e[i] > 0)
            lower = tuple(p - (i == axis) for i, p in enumerate(e))
            before = made[lower]
            made[e] = at[axis] * weight if before is None else before * at[axis]
            values.append(made[e])
        total = values if total is None else [x + y for x, y in zip(total, values)]
    return [jnp.ones_like(middle[0])] + total


def pair_products(quads, tensors):
    q_high, q_low = split(jnp.concatenate(quads, axis=0))
    t_high, t_low = split(jnp.concatenate(tensors + [jnp.zeros((56, 128), F32)], axis=0))
    left = jnp.concatenate([q_high, q_low], axis=1)
    right = jnp.concatenate([t_high, t_low], axis=0)
    both = dot(left, jnp.concatenate([right, right], axis=1), NT)
    return both[:, :128] + both[:, 128:]


def gather_same(products, same, spread, lane):
    sides = []
    for one in products:
        kept = (one.reshape(MONOS, 8, 128) * same).reshape(8 * MONOS, 128)
        sides.append(jnp.concatenate(split(kept), axis=1))
    spreaded = dot(jnp.concatenate(sides, axis=0), spread, NN)
    groups = []
    for g in range(len(products)):
        tiles = []
        for first in (0, 14, 28):
            count = min(14, MONOS - first)
            tile = jnp.zeros((8, 128), F32)
            for k in reversed(range(count)):
                at = 8 * (MONOS * g + first + k)
                tile = jnp.where(lane < 9 * k + 9, spreaded[at : at + 8], tile)
            tiles.append(tile)
        groups.append(tiles)
    return groups


def column(row):
    return jnp.transpose(jnp.broadcast_to(row, (128, 128)))


def kernel(
    devices, low_size, cap,
    seg_hbm, leaf_hbm, perm_hbm, spread_hbm, count_hbm, offset_hbm,
    leaf_out, root_out,
    seg_ref, leaf_ref, perm_ref, spread_ref, count_ref, offset_ref,
    place, moments, acc, sbuf, rbuf, root_send, root_recv,
    leaf_made, root_made,
    load_sem, send_sem, recv_sem, root_send_sem, root_recv_sem, out_sem,
):
    blocks = seg_ref.shape[1]
    eighth = blocks // 8
    pieces = [pl.ds(0, 2 * eighth), pl.ds(6 * eighth, 2 * eighth), pl.ds(2 * eighth, 4 * eighth)]
    fetches = [
        pltpu.make_async_copy(src, dst, load_sem.at[i])
        for i, (src, dst) in enumerate(
            [(leaf_hbm, leaf_ref)]
            + [(seg_hbm.at[:, p], seg_ref.at[:, p]) for p in pieces[:2]]
            + [(spread_hbm, spread_ref), (count_hbm, count_ref), (offset_hbm, offset_ref)]
            + [(seg_hbm.at[:, pieces[2]], seg_ref.at[:, pieces[2]]), (perm_hbm, perm_ref)]
        )
    ]
    for fetch in fetches:
        fetch.start()

    me = lax.axis_index("top") * low_size + lax.axis_index("low")

    def partner(step):
        other = lax.rem(me + step, devices)
        return other, (other // low_size, lax.rem(other, low_size))

    barrier = pltpu.get_barrier_semaphore()

    def greet(step, carry):
        pl.semaphore_signal(barrier, inc=1, device_id=partner(step)[1], device_id_type=MESH)
        return carry

    lax.fori_loop(1, devices, greet, 0)
    moments[...] = jnp.zeros_like(moments)
    acc[...] = jnp.zeros_like(acc)

    fetches[0].wait()
    leaves = leaf_ref[...]
    for chunk in range(blocks // 128):
        place[3, chunk * 128 : chunk * 128 + 128] = column(
            leaves[chunk : chunk + 1].astype(F32)
        )
    for fetch in fetches[1:6]:
        fetch.wait()

    lane8 = lax.broadcasted_iota(jnp.int32, (8, 128), 1)
    row8 = lax.broadcasted_iota(jnp.int32, (8, 128), 0)
    same = jnp.where(lax.rem(lane8, 8) == row8, 1.0, 0.0)

    def load(group):
        rows = pl.ds(pl.multiple_of(group * 8, 8), 8)
        parts = [seg_ref[c, rows, :] for c in range(9)]
        scaled = [h * (2.0 / math.sqrt(128.0)) for h in parts[6:9]]
        tensors = [b * h for b in parts[0:3] for h in scaled]
        return rows, parts[3:6], parts[6:9], tensors

    def p2m(first_group):
        def body(turn, carry):
            products, places = [], []
            for u in range(TOGETHER):
                rows, middle, half, tensors = load(first_group + turn * TOGETHER + u)
                products.append(pair_products(monomials(middle, half), tensors))
                places.append(rows)
            for rows, tiles in zip(places, gather_same(products, same, spread_ref[...], lane8)):
                moments[0, rows, :] = tiles[0]
                moments[1, rows, :] = tiles[1]
                moments[2, rows, :] = jnp.where(lane8 == 63, place[3, rows, :], tiles[2])
            return carry

        return body

    lane16 = lax.broadcasted_iota(jnp.int32, (SLOTS, 128), 1)
    slot16 = lax.broadcasted_iota(jnp.int32, (SLOTS, 128), 0)

    def packed(owner):
        rows = pl.ds(offset_ref[0, owner], SLOTS)
        dead = (lane16 == 63) & (slot16 >= count_ref[0, owner])
        third = jnp.where(dead, -1.0, moments[2, rows, :])
        folded = jnp.where(lane8 < 64, third[:8], pltpu.roll(third[8:], 64, 1))
        return moments[0, rows, :], moments[1, rows, :], folded

    def put(ref, step, pieces):
        ref[step, 0:SLOTS, :] = pieces[0]
        ref[step, SLOTS : 2 * SLOTS, :] = pieces[1]
        ref[step, 2 * SLOTS : ROWS, :] = pieces[2]

    def block_copy(step):
        return pltpu.make_async_remote_copy(
            src_ref=sbuf.at[step], dst_ref=rbuf.at[step],
            send_sem=send_sem.at[step], recv_sem=recv_sem.at[step],
            device_id=partner(step)[1], device_id_type=MESH,
        )

    def root_copy(step):
        return pltpu.make_async_remote_copy(
            src_ref=root_send, dst_ref=root_recv.at[step],
            send_sem=root_send_sem.at[step], recv_sem=root_recv_sem.at[step],
            device_id=partner(step)[1], device_id_type=MESH,
        )

    ready = eighth // cap
    turns = eighth // (8 * TOGETHER)

    def send_early(done):
        def body(turn, carry):
            spot = lax.rem(me + turn, 2 * ready)
            owner = jnp.where(spot < ready, spot + done, devices - 2 * ready + spot - done)
            step = lax.rem(owner - me + devices, devices)

            @pl.when(step != 0)
            def _():
                put(sbuf, step, packed(owner))
                block_copy(step).start()

            return carry

        return body

    lax.fori_loop(0, turns, p2m(0), 0)
    lax.fori_loop(0, turns, p2m(7 * eighth // 8), 0)
    pl.semaphore_wait(barrier, devices - 1)
    lax.fori_loop(0, 2 * ready, send_early(0), 0)
    lax.fori_loop(0, turns, p2m(eighth // 8), 0)
    lax.fori_loop(0, turns, p2m(6 * eighth // 8), 0)
    lax.fori_loop(0, 2 * ready, send_early(ready), 0)
    fetches[6].wait()
    lax.fori_loop(0, 4 * turns, p2m(2 * eighth // 8), 0)

    def send_late(step, carry):
        owner = partner(step)[0]

        @pl.when((owner >= 2 * ready) & (owner < devices - 2 * ready))
        def _():
            put(sbuf, step, packed(owner))
            block_copy(step).start()

        return carry

    lax.fori_loop(1, devices, send_late, 0)
    put(rbuf, 0, packed(me))

    levels = LEAF_DEV.bit_length() - 1 + devices.bit_length() - 1
    depth = [len(range(d, levels, 3)) for d in range(3)]
    for chunk in range(blocks // 128):
        index = lax.broadcasted_iota(jnp.int32, (1, 128), 1) + chunk * 128
        owner = jnp.zeros((1, 128), jnp.int32)
        for o in range(devices):
            end = offset_ref[0, o] + count_ref[0, o]
            owner = owner + jnp.where(index >= end, 1, 0)
        cell = owner * LEAF_DEV + leaves[chunk : chunk + 1]
        for d in range(3):
            centre = jnp.zeros((1, 128), F32)
            for level in range(d, levels, 3):
                bit = lax.shift_right_logical(cell, level) & 1
                centre = centre + jnp.where(bit == 1, 1.0, -1.0) * 2.0 ** (level // 3)
            place[d, chunk * 128 : chunk * 128 + 128] = column(centre)

    def to_root(turn, carry):
        shrink = [0.5**k for k in depth]
        total = None
        for u in range(2):
            rows, middle, half, tensors = load(turn * 2 + u)
            middle = [(p + place[d, rows, :]) * shrink[d] for d, p in enumerate(middle)]
            half = [h * shrink[d] for d, h in enumerate(half)]
            products = pair_products(monomials(middle, half), tensors)
            total = products if total is None else total + products
        acc[...] += total
        return carry

    lax.fori_loop(0, blocks // 16, to_root, 0)
    (tiles,) = gather_same([acc[...] * 2.0 ** (-levels / 2)], same, spread_ref[...], lane8)
    own = jnp.concatenate(
        [jnp.sum(t, axis=0, keepdims=True) for t in tiles] + [jnp.zeros((1, 128), F32)], axis=0
    )
    root_send[...] = own

    def send_root(step, carry):
        root_copy(step).start()
        return carry

    lax.fori_loop(1, devices, send_root, 0)

    def take(step, carry):
        block_copy(step).wait()
        return carry

    cells = jnp.zeros((LEAF_DEV, 384), F32)
    bounds = [0, devices // 2, devices // 8 * 7, devices]
    for start, end in zip(bounds[:-1], bounds[1:]):
        lax.fori_loop(max(start, 1), end, take, 0)
        rows = (end - start) * 8
        leaf_lane = lax.broadcasted_iota(jnp.int32, (rows, 128), 1).astype(F32)
        got = [
            rbuf[start:end, at : at + 8].reshape(rows, 128) for at in range(0, ROWS, 8)
        ]
        for side in (got[0::2], [got[1], got[3], pltpu.roll(got[4], 64, 1)]):
            hit = jnp.where(side[2][:, 63:64] == leaf_lane, 1.0, 0.0)
            hit = jnp.transpose(hit).astype(BF16)
            high, low = split(jnp.concatenate(side, axis=1))
            cells = cells + dot(hit, high, NN) + dot(hit, low, NN)
    fetches[7].wait()
    perm = perm_ref[...]
    high, low = split(cells)
    leaf_made[...] = (dot(perm, high, NT) + dot(perm, low, NT))[:COEFFS]
    leaf_store = pltpu.make_async_copy(leaf_made, leaf_out, out_sem.at[0])
    leaf_store.start()

    def take_root(step, carry):
        root_copy(step).wait()
        return carry

    lax.fori_loop(1, devices, take_root, 0)
    root_recv[0] = own
    total = jnp.sum(root_recv[...], axis=0)
    line = jnp.concatenate([total[0:1], total[1:2], total[2:3]], axis=1)
    high, low = split(jnp.broadcast_to(line, (16, 384)))
    root_made[...] = (dot(high, perm, NT) + dot(low, perm, NT))[0:1, :COEFFS]
    root_store = pltpu.make_async_copy(root_made, root_out, out_sem.at[1])
    root_store.start()
    leaf_store.wait()
    root_store.wait()


def hand_over(leaf_in, root_in, leaf_out, root_out, sem):
    cuts = [0, 80, 160, 240, COEFFS]
    copies = [
        pltpu.make_async_copy(leaf_in.at[a:b], leaf_out.at[a:b], sem.at[i])
        for i, (a, b) in enumerate(zip(cuts[:-1], cuts[1:]))
    ]
    copies.append(pltpu.make_async_copy(root_in, root_out, sem.at[4]))
    for copy in copies:
        copy.start()
    for copy in copies:
        copy.wait()


def local(devices, low_size, segments, send_counts, send_offsets, leaf_of_block):
    blocks = segments.shape[0]
    lanes = np.arange(128)
    one = ((lanes[None, :] % 9 == lanes[:, None] // 8) & (lanes[:, None] < 72)).astype(np.float32)
    spread = jnp.asarray(np.concatenate([one, one], axis=0), BF16)
    perm = jnp.asarray(make_permutation(), BF16)
    hbm = pl.BlockSpec(memory_space=pltpu.HBM)
    cap = max(2, 2 * blocks // devices)
    dma = pltpu.SemaphoreType.DMA
    shapes = (
        jax.ShapeDtypeStruct((COEFFS, LEAF_DEV), F32),
        jax.ShapeDtypeStruct((1, COEFFS), F32),
    )
    results = pl.pallas_call(
        functools.partial(kernel, devices, low_size, cap),
        out_shape=shapes,
        in_specs=[hbm] * 6,
        out_specs=(hbm, hbm),
        scratch_shapes=[
            pltpu.VMEM((9, blocks, 128), F32),
            pltpu.VMEM((blocks // 128, 128), jnp.int32),
            pltpu.VMEM((320, 384), BF16),
            pltpu.VMEM((256, 128), BF16),
            pltpu.SMEM((1, devices), jnp.int32),
            pltpu.SMEM((1, devices), jnp.int32),
            pltpu.VMEM((4, blocks, 128), F32),
            pltpu.VMEM((3, blocks + SLOTS, 128), F32),
            pltpu.VMEM((8 * MONOS, 128), F32),
            pltpu.VMEM((devices, ROWS, 128), F32),
            pltpu.VMEM((devices, ROWS, 128), F32),
            pltpu.VMEM((4, 128), F32),
            pltpu.VMEM((devices, 4, 128), F32),
            pltpu.VMEM((COEFFS, LEAF_DEV), F32),
            pltpu.VMEM((1, COEFFS), F32),
            dma((8,)),
            dma((devices,)),
            dma((devices,)),
            dma((devices,)),
            dma((devices,)),
            dma((2,)),
        ],
        compiler_params=pltpu.CompilerParams(
            collective_id=0, has_side_effects=True, vmem_limit_bytes=63 * 1024 * 1024
        ),
        cost_estimate=pl.CostEstimate(
            flops=2 * blocks * 128 * COEFFS * 2, bytes_accessed=blocks * 128 * 40, transcendentals=0
        ),
    )(
        jnp.transpose(segments, (1, 0, 2)),
        leaf_of_block.reshape(blocks // 128, 128),
        perm,
        spread,
        send_counts,
        send_offsets,
    )
    return pl.pallas_call(
        hand_over,
        out_shape=shapes,
        in_specs=[hbm, hbm],
        out_specs=(hbm, hbm),
        scratch_shapes=[dma((5,))],
        compiler_params=pltpu.CompilerParams(vmem_limit_bytes=63 * 1024 * 1024),
    )(*results)


def solution(mesh):
    placed = (
        P(("top", "low"), None, None),
        P(("top", "low"), None),
        P(("top", "low"), None),
        P(("top", "low")),
    )
    return jax.shard_map(
        functools.partial(local, mesh.size, mesh.shape["low"]),
        mesh=mesh,
        in_specs=placed,
        out_specs=(P(None, ("top", "low")), P(("top", "low"), None)),
        check_vma=False,
    )
```

```python
import functools
import math

import jax
import jax.numpy as jnp
import numpy as np
from jax import lax
from jax.experimental import pallas as pl
from jax.experimental.pallas import tpu as pltpu
from jax.sharding import PartitionSpec as P

MONOS = 35
COEFFS = 315
LEAF_DEV = 128
SLOTS = 16
ROWS = 2 * SLOTS + SLOTS // 2
MESH = pl.DeviceIdType.MESH
BF16 = jnp.bfloat16
F32 = jnp.float32
NT = (((1,), (1,)), ((), ()))
NN = (((1,), (0,)), ((), ()))


def make_exponents():
    collected = []
    for degree_total in range(5):
        for first_power in range(degree_total, -1, -1):
            for second_power in range(degree_total - first_power, -1, -1):
                collected.append(
                    (first_power, second_power, degree_total - first_power - second_power)
                )
    return collected


EXPONENTS = make_exponents()
POINTS = (
    (-math.sqrt(0.6), 5.0 / 18.0),
    (0.0, 8.0 / 18.0),
    (math.sqrt(0.6), 5.0 / 18.0),
)


def make_permutation():
    table = np.zeros((320, 384), np.float32)
    for m in range(MONOS):
        for a in range(9):
            table[MONOS * a + m, 128 * (m // 14) + 9 * (m % 14) + a] = 1.0
    return table


def split(x):
    high = x.astype(BF16)
    low = (x - high.astype(F32)).astype(BF16)
    return high, low


def dot(a, b, dims):
    return lax.dot_general(a, b, dims, preferred_element_type=F32)


def monomials(middle, half):
    total = None
    for point, weight in POINTS:
        at = [m + point * h if point else m for m, h in zip(middle, half)]
        made = {(0, 0, 0): None}
        values = []
        for e in EXPONENTS[1:]:
            axis = next(i for i in range(3) if e[i] > 0)
            lower = tuple(p - (i == axis) for i, p in enumerate(e))
            before = made[lower]
            made[e] = at[axis] * weight if before is None else before * at[axis]
            values.append(made[e])
        total = values if total is None else [x + y for x, y in zip(total, values)]
    return [jnp.ones_like(middle[0])] + total


def pair_products(quads, tensors):
    q_high, q_low = split(jnp.concatenate(quads, axis=0))
    t_high, t_low = split(jnp.concatenate(tensors + [jnp.zeros((56, 128), F32)], axis=0))
    left = jnp.concatenate([q_high, q_low], axis=1)
    right = jnp.concatenate([t_high, t_low], axis=0)
    both = dot(left, jnp.concatenate([right, right], axis=1), NT)
    return both[:, :128] + both[:, 128:]


def gather_same(products, same, spread, lane):
    sides = []
    for one in products:
        kept = (one.reshape(MONOS, 8, 128) * same).reshape(8 * MONOS, 128)
        sides.append(jnp.concatenate(split(kept), axis=1))
    spreaded = dot(jnp.concatenate(sides, axis=0), spread, NN)
    groups = []
    for g in range(len(products)):
        tiles = []
        for first in (0, 14, 28):
            count = min(14, MONOS - first)
            tile = jnp.zeros((8, 128), F32)
            for k in reversed(range(count)):
                at = 8 * (MONOS * g + first + k)
                tile = jnp.where(lane < 9 * k + 9, spreaded[at : at + 8], tile)
            tiles.append(tile)
        groups.append(tiles)
    return groups


def column(row):
    return jnp.transpose(jnp.broadcast_to(row, (128, 128)))


def kernel(
    devices, low_size,
    seg_hbm, leaf_hbm, perm_hbm, spread_hbm, count_hbm, offset_hbm,
    leaf_out, root_out,
    seg_ref, leaf_ref, perm_ref, spread_ref, count_ref, offset_ref,
    place, acc, sbuf, rbuf, root_send, root_recv,
    leaf_made, root_made,
    load_sem, send_sem, recv_sem, root_send_sem, root_recv_sem, out_sem,
):
    blocks = seg_ref.shape[1] - SLOTS
    body_rows = pl.ds(0, blocks)
    fetches = [
        pltpu.make_async_copy(src, dst, load_sem.at[i])
        for i, (src, dst) in enumerate(
            (
                (leaf_hbm, leaf_ref),
                (seg_hbm, seg_ref.at[:, body_rows]),
                (spread_hbm, spread_ref),
                (count_hbm, count_ref),
                (offset_hbm, offset_ref),
                (perm_hbm, perm_ref),
            )
        )
    ]
    for fetch in fetches:
        fetch.start()

    me = lax.axis_index("top") * low_size + lax.axis_index("low")

    def partner(step):
        other = lax.rem(me + step, devices)
        return other, (other // low_size, lax.rem(other, low_size))

    barrier = pltpu.get_barrier_semaphore()

    def greet(step, carry):
        pl.semaphore_signal(barrier, inc=1, device_id=partner(step)[1], device_id_type=MESH)
        return carry

    lax.fori_loop(1, devices, greet, 0)
    seg_ref[:, blocks:] = jnp.zeros((9, SLOTS, 128), F32)
    place[:, blocks:] = jnp.zeros((4, SLOTS, 128), F32)
    acc[...] = jnp.zeros_like(acc)

    fetches[0].wait()
    leaves = leaf_ref[...]
    for chunk in range(blocks // 128):
        place[3, chunk * 128 : chunk * 128 + 128] = column(
            leaves[chunk : chunk + 1].astype(F32)
        )
    for fetch in fetches[1:5]:
        fetch.wait()

    lane8 = lax.broadcasted_iota(jnp.int32, (8, 128), 1)
    row8 = lax.broadcasted_iota(jnp.int32, (8, 128), 0)
    same = jnp.where(lax.rem(lane8, 8) == row8, 1.0, 0.0)

    def load(rows):
        parts = [seg_ref[c, rows, :] for c in range(9)]
        scaled = [h * (2.0 / math.sqrt(128.0)) for h in parts[6:9]]
        tensors = [b * h for b in parts[0:3] for h in scaled]
        return parts[3:6], parts[6:9], tensors

    def block_copy(step):
        return pltpu.make_async_remote_copy(
            src_ref=sbuf.at[step], dst_ref=rbuf.at[step],
            send_sem=send_sem.at[step], recv_sem=recv_sem.at[step],
            device_id=partner(step)[1], device_id_type=MESH,
        )

    def root_copy(step):
        return pltpu.make_async_remote_copy(
            src_ref=root_send, dst_ref=root_recv.at[step],
            send_sem=root_send_sem.at[step], recv_sem=root_recv_sem.at[step],
            device_id=partner(step)[1], device_id_type=MESH,
        )

    pl.semaphore_wait(barrier, devices - 1)

    def send(turn, carry):
        steps, products, leaf_rows = [], [], []
        for u in range(2):
            step = lax.rem(turn * 2 + u + 1, devices)
            owner = partner(step)[0]
            for side in (0, 8):
                rows = pl.ds(offset_ref[0, owner] + side, 8)
                middle, half, tensors = load(rows)
                products.append(pair_products(monomials(middle, half), tensors))
                leaf = jnp.where(row8 + side < count_ref[0, owner], place[3, rows, :], -1.0)
                leaf_rows.append(leaf)
            steps.append(step)
        made = gather_same(products, same, spread_ref[...], lane8)
        for u, step in enumerate(steps):
            near, far = made[2 * u : 2 * u + 2]
            last_near = jnp.where(lane8 == 63, leaf_rows[2 * u], near[2])
            last_far = jnp.where(lane8 == 63, leaf_rows[2 * u + 1], far[2])
            sbuf[step, 0:8, :] = near[0]
            sbuf[step, 8:16, :] = far[0]
            sbuf[step, 16:24, :] = near[1]
            sbuf[step, 24:32, :] = far[1]
            sbuf[step, 32:40, :] = jnp.where(lane8 < 64, last_near, pltpu.roll(last_far, 64, 1))

            @pl.when(step != 0)
            def _():
                block_copy(step).start()

        return carry

    lax.fori_loop(0, devices // 2, send, 0)
    rbuf[0] = sbuf[0]

    levels = LEAF_DEV.bit_length() - 1 + devices.bit_length() - 1
    depth = [len(range(d, levels, 3)) for d in range(3)]
    for chunk in range(blocks // 128):
        index = lax.broadcasted_iota(jnp.int32, (1, 128), 1) + chunk * 128
        owner = jnp.zeros((1, 128), jnp.int32)
        for o in range(devices):
            end = offset_ref[0, o] + count_ref[0, o]
            owner = owner + jnp.where(index >= end, 1, 0)
        cell = owner * LEAF_DEV + leaves[chunk : chunk + 1]
        for d in range(3):
            centre = jnp.zeros((1, 128), F32)
            for level in range(d, levels, 3):
                bit = lax.shift_right_logical(cell, level) & 1
                centre = centre + jnp.where(bit == 1, 1.0, -1.0) * 2.0 ** (level // 3)
            place[d, chunk * 128 : chunk * 128 + 128] = column(centre)

    def to_root(turn, carry):
        shrink = [0.5**k for k in depth]
        total = None
        for u in range(2):
            rows = pl.ds(pl.multiple_of(turn * 16 + u * 8, 8), 8)
            middle, half, tensors = load(rows)
            middle = [(p + place[d, rows, :]) * shrink[d] for d, p in enumerate(middle)]
            half = [h * shrink[d] for d, h in enumerate(half)]
            products = pair_products(monomials(middle, half), tensors)
            total = products if total is None else total + products
        acc[...] += total
        return carry

    lax.fori_loop(0, blocks // 16, to_root, 0)
    (tiles,) = gather_same([acc[...] * 2.0 ** (-levels / 2)], same, spread_ref[...], lane8)
    own = jnp.concatenate(
        [jnp.sum(t, axis=0, keepdims=True) for t in tiles] + [jnp.zeros((1, 128), F32)], axis=0
    )
    root_send[...] = own

    def send_root(step, carry):
        root_copy(step).start()
        return carry

    lax.fori_loop(1, devices, send_root, 0)

    def take(step, carry):
        block_copy(step).wait()
        return carry

    cells = jnp.zeros((LEAF_DEV, 384), F32)
    bounds = [0, devices // 2, devices // 8 * 7, devices]
    for start, end in zip(bounds[:-1], bounds[1:]):
        lax.fori_loop(max(start, 1), end, take, 0)
        rows = (end - start) * 8
        leaf_lane = lax.broadcasted_iota(jnp.int32, (rows, 128), 1).astype(F32)
        got = [
            rbuf[start:end, at : at + 8].reshape(rows, 128) for at in range(0, ROWS, 8)
        ]
        for side in (got[0::2], [got[1], got[3], pltpu.roll(got[4], 64, 1)]):
            hit = jnp.where(side[2][:, 63:64] == leaf_lane, 1.0, 0.0)
            hit = jnp.transpose(hit).astype(BF16)
            high, low = split(jnp.concatenate(side, axis=1))
            cells = cells + dot(hit, high, NN) + dot(hit, low, NN)
    fetches[5].wait()
    perm = perm_ref[...]
    high, low = split(cells)
    leaf_made[...] = (dot(perm, high, NT) + dot(perm, low, NT))[:COEFFS]
    leaf_store = pltpu.make_async_copy(leaf_made, leaf_out, out_sem.at[0])
    leaf_store.start()

    def take_root(step, carry):
        root_copy(step).wait()
        return carry

    lax.fori_loop(1, devices, take_root, 0)
    root_recv[0] = own
    total = jnp.sum(root_recv[...], axis=0)
    line = jnp.concatenate([total[0:1], total[1:2], total[2:3]], axis=1)
    high, low = split(jnp.broadcast_to(line, (16, 384)))
    root_made[...] = (dot(high, perm, NT) + dot(low, perm, NT))[0:1, :COEFFS]
    root_store = pltpu.make_async_copy(root_made, root_out, out_sem.at[1])
    root_store.start()
    leaf_store.wait()
    root_store.wait()


def hand_over(leaf_in, root_in, leaf_out, root_out, leaf_held, root_held, sem):
    incoming = [
        pltpu.make_async_copy(leaf_in, leaf_held, sem.at[0]),
        pltpu.make_async_copy(root_in, root_held, sem.at[1]),
    ]
    outgoing = [
        pltpu.make_async_copy(leaf_held, leaf_out, sem.at[2]),
        pltpu.make_async_copy(root_held, root_out, sem.at[3]),
    ]
    for copy in incoming:
        copy.start()
    for first, then in zip(incoming, outgoing):
        first.wait()
        then.start()
    for copy in outgoing:
        copy.wait()


def local(devices, low_size, segments, send_counts, send_offsets, leaf_of_block):
    blocks = segments.shape[0]
    lanes = np.arange(128)
    one = ((lanes[None, :] % 9 == lanes[:, None] // 8) & (lanes[:, None] < 72)).astype(np.float32)
    spread = jnp.asarray(np.concatenate([one, one], axis=0), BF16)
    perm = jnp.asarray(make_permutation(), BF16)
    hbm = pl.BlockSpec(memory_space=pltpu.HBM)
    dma = pltpu.SemaphoreType.DMA
    shapes = (
        jax.ShapeDtypeStruct((COEFFS, LEAF_DEV), F32),
        jax.ShapeDtypeStruct((1, COEFFS), F32),
    )
    results = pl.pallas_call(
        functools.partial(kernel, devices, low_size),
        out_shape=shapes,
        in_specs=[hbm] * 6,
        out_specs=(hbm, hbm),
        scratch_shapes=[
            pltpu.VMEM((9, blocks + SLOTS, 128), F32),
            pltpu.VMEM((blocks // 128, 128), jnp.int32),
            pltpu.VMEM((320, 384), BF16),
            pltpu.VMEM((256, 128), BF16),
            pltpu.SMEM((1, devices), jnp.int32),
            pltpu.SMEM((1, devices), jnp.int32),
            pltpu.VMEM((4, blocks + SLOTS, 128), F32),
            pltpu.VMEM((8 * MONOS, 128), F32),
            pltpu.VMEM((devices, ROWS, 128), F32),
            pltpu.VMEM((devices, ROWS, 128), F32),
            pltpu.VMEM((4, 128), F32),
            pltpu.VMEM((devices, 4, 128), F32),
            pltpu.VMEM((COEFFS, LEAF_DEV), F32),
            pltpu.VMEM((1, COEFFS), F32),
            dma((6,)),
            dma((devices,)),
            dma((devices,)),
            dma((devices,)),
            dma((devices,)),
            dma((2,)),
        ],
        compiler_params=pltpu.CompilerParams(
            collective_id=0, has_side_effects=True, vmem_limit_bytes=63 * 1024 * 1024
        ),
        cost_estimate=pl.CostEstimate(
            flops=2 * blocks * 128 * COEFFS * 2, bytes_accessed=blocks * 128 * 40, transcendentals=0
        ),
    )(
        jnp.transpose(segments, (1, 0, 2)),
        leaf_of_block.reshape(blocks // 128, 128),
        perm,
        spread,
        send_counts,
        send_offsets,
    )
    return pl.pallas_call(
        hand_over,
        out_shape=shapes,
        in_specs=[hbm, hbm],
        out_specs=(hbm, hbm),
        scratch_shapes=[
            pltpu.VMEM((COEFFS, LEAF_DEV), F32),
            pltpu.VMEM((1, COEFFS), F32),
            dma((4,)),
        ],
        compiler_params=pltpu.CompilerParams(vmem_limit_bytes=63 * 1024 * 1024),
    )(*results)


def solution(mesh):
    placed = (
        P(("top", "low"), None, None),
        P(("top", "low"), None),
        P(("top", "low"), None),
        P(("top", "low")),
    )
    return jax.shard_map(
        functools.partial(local, mesh.size, mesh.shape["low"]),
        mesh=mesh,
        in_specs=placed,
        out_specs=(P(None, ("top", "low")), P(("top", "low"), None)),
        check_vma=False,
    )
```

```python
import functools
import math

import jax
import jax.numpy as jnp
import numpy as np
from jax import lax
from jax.experimental import pallas as pl
from jax.experimental.pallas import tpu as pltpu
from jax.sharding import PartitionSpec as P

MONOS = 35
COEFFS = 315
LEAF_DEV = 128
SLOTS = 16
ROWS = 2 * SLOTS + SLOTS // 2
MESH = pl.DeviceIdType.MESH
BF16 = jnp.bfloat16
F32 = jnp.float32
NT = (((1,), (1,)), ((), ()))
NN = (((1,), (0,)), ((), ()))


def make_exponents():
    collected = []
    for degree_total in range(5):
        for first_power in range(degree_total, -1, -1):
            for second_power in range(degree_total - first_power, -1, -1):
                collected.append(
                    (first_power, second_power, degree_total - first_power - second_power)
                )
    return collected


EXPONENTS = make_exponents()
POINTS = (
    (-math.sqrt(0.6), 5.0 / 18.0),
    (0.0, 8.0 / 18.0),
    (math.sqrt(0.6), 5.0 / 18.0),
)


def make_permutation():
    table = np.zeros((320, 384), np.float32)
    for m in range(MONOS):
        for a in range(9):
            table[MONOS * a + m, 128 * (m // 14) + 9 * (m % 14) + a] = 1.0
    return table


def make_shift_tiles(depth, scale):
    tiles, places = [], []
    for target in EXPONENTS:
        table = np.zeros((40, 384), np.float32)
        for n, source in enumerate(EXPONENTS):
            rest = tuple(t - s for t, s in zip(target, source))
            if min(rest) < 0:
                continue
            factor = scale
            for t, s, d in zip(target, source, depth):
                factor *= math.comb(t, s) * 2.0 ** (-d * s)
            lane = 128 * (n // 14) + 9 * (n % 14)
            table[EXPONENTS.index(rest), lane : lane + 9] = factor
        found = []
        for i in range(5):
            for j in range(3):
                tile = table[8 * i : 8 * i + 8, 128 * j : 128 * j + 128]
                if tile.any():
                    found.append((i, j, len(tiles)))
                    tiles.append(tile)
        places.append(found)
    return np.stack(tiles), places


def split(x):
    high = x.astype(BF16)
    low = (x - high.astype(F32)).astype(BF16)
    return high, low


def dot(a, b, dims):
    return lax.dot_general(a, b, dims, preferred_element_type=F32)


def monomials(middle, half):
    total = None
    for point, weight in POINTS:
        at = [m + point * h if point else m for m, h in zip(middle, half)]
        made = {(0, 0, 0): None}
        values = []
        for e in EXPONENTS[1:]:
            axis = next(i for i in range(3) if e[i] > 0)
            lower = tuple(p - (i == axis) for i, p in enumerate(e))
            before = made[lower]
            made[e] = at[axis] * weight if before is None else before * at[axis]
            values.append(made[e])
        total = values if total is None else [x + y for x, y in zip(total, values)]
    return [jnp.ones_like(middle[0])] + total


def pair_products(quads, tensors):
    q_high, q_low = split(jnp.concatenate(quads, axis=0))
    stacked = jnp.concatenate(tensors + [jnp.zeros((56, 128), F32)], axis=0)
    right = jnp.concatenate(split(jnp.transpose(stacked)), axis=1)
    left = jnp.concatenate([q_high, q_low], axis=1)
    both = dot(left, jnp.concatenate([right, right], axis=0), NN)
    return both[:, :128] + both[:, 128:]


def gather_same(products, same, spread, lane):
    sides = []
    for one in products:
        kept = (one.reshape(MONOS, 8, 128) * same).reshape(8 * MONOS, 128)
        sides.append(jnp.concatenate(split(kept), axis=1))
    spreaded = dot(jnp.concatenate(sides, axis=0), spread, NN)
    groups = []
    for g in range(len(products)):
        tiles = []
        for first in (0, 14, 28):
            count = min(14, MONOS - first)
            tile = jnp.zeros((8, 128), F32)
            for k in reversed(range(count)):
                at = 8 * (MONOS * g + first + k)
                tile = jnp.where(lane < 9 * k + 9, spreaded[at : at + 8], tile)
            tiles.append(tile)
        groups.append(tiles)
    return groups


def column(row):
    return jnp.transpose(jnp.broadcast_to(row, (128, 128)))


def kernel(
    devices, low_size, depth, tile_places,
    seg_hbm, leaf_hbm, perm_hbm, spread_hbm, count_hbm, offset_hbm, shift_hbm, power_hbm,
    leaf_out, root_out,
    seg_ref, leaf_ref, perm_ref, spread_ref, count_ref, offset_ref, shift_ref, power_ref,
    place, sbuf, rbuf, root_send, root_recv,
    leaf_made, root_made,
    load_sem, send_sem, recv_sem, root_send_sem, root_recv_sem, out_sem,
):
    blocks = seg_ref.shape[1] - SLOTS
    body_rows = pl.ds(0, blocks)
    fetches = [
        pltpu.make_async_copy(src, dst, load_sem.at[i])
        for i, (src, dst) in enumerate(
            (
                (leaf_hbm, leaf_ref),
                (seg_hbm, seg_ref.at[:, body_rows]),
                (spread_hbm, spread_ref),
                (count_hbm, count_ref),
                (offset_hbm, offset_ref),
                (perm_hbm, perm_ref),
                (shift_hbm, shift_ref),
                (power_hbm, power_ref),
            )
        )
    ]
    for fetch in fetches:
        fetch.start()

    me = lax.axis_index("top") * low_size + lax.axis_index("low")

    def partner(step):
        other = lax.rem(me + step, devices)
        return other, (other // low_size, lax.rem(other, low_size))

    barrier = pltpu.get_barrier_semaphore()

    def greet(step, carry):
        pl.semaphore_signal(barrier, inc=1, device_id=partner(step)[1], device_id_type=MESH)
        return carry

    lax.fori_loop(1, devices, greet, 0)
    seg_ref[:, blocks:] = jnp.zeros((9, SLOTS, 128), F32)
    place[blocks:] = jnp.zeros((SLOTS, 128), F32)

    fetches[0].wait()
    leaves = leaf_ref[...]
    for chunk in range(blocks // 128):
        place[chunk * 128 : chunk * 128 + 128] = column(
            leaves[chunk : chunk + 1].astype(F32)
        )
    for fetch in fetches[1:5]:
        fetch.wait()

    lane8 = lax.broadcasted_iota(jnp.int32, (8, 128), 1)
    row8 = lax.broadcasted_iota(jnp.int32, (8, 128), 0)
    same = jnp.where(lax.rem(lane8, 8) == row8, 1.0, 0.0)

    def load(rows):
        parts = [seg_ref[c, rows, :] for c in range(9)]
        scaled = [h * (2.0 / math.sqrt(128.0)) for h in parts[6:9]]
        tensors = [b * h for b in parts[0:3] for h in scaled]
        return parts[3:6], parts[6:9], tensors

    def block_copy(step):
        return pltpu.make_async_remote_copy(
            src_ref=sbuf.at[step], dst_ref=rbuf.at[step],
            send_sem=send_sem.at[step], recv_sem=recv_sem.at[step],
            device_id=partner(step)[1], device_id_type=MESH,
        )

    def root_copy(step):
        return pltpu.make_async_remote_copy(
            src_ref=root_send, dst_ref=root_recv.at[step],
            send_sem=root_send_sem.at[step], recv_sem=root_recv_sem.at[step],
            device_id=partner(step)[1], device_id_type=MESH,
        )

    pl.semaphore_wait(barrier, devices - 1)

    def send(turn, carry):
        steps, products, leaf_rows = [], [], []
        for u in range(2):
            step = lax.rem(turn * 2 + u + 1, devices)
            owner = partner(step)[0]
            for side in (0, 8):
                rows = pl.ds(offset_ref[0, owner] + side, 8)
                middle, half, tensors = load(rows)
                products.append(pair_products(monomials(middle, half), tensors))
                leaf = jnp.where(row8 + side < count_ref[0, owner], place[rows, :], -1.0)
                leaf_rows.append(leaf)
            steps.append(step)
        made = gather_same(products, same, spread_ref[0], lane8)
        for u, step in enumerate(steps):
            near, far = made[2 * u : 2 * u + 2]
            last_near = jnp.where(lane8 == 63, leaf_rows[2 * u], near[2])
            last_far = jnp.where(lane8 == 63, leaf_rows[2 * u + 1], far[2])
            sbuf[step, 0:8, :] = near[0]
            sbuf[step, 8:16, :] = far[0]
            sbuf[step, 16:24, :] = near[1]
            sbuf[step, 24:32, :] = far[1]
            sbuf[step, 32:40, :] = jnp.where(lane8 < 64, last_near, pltpu.roll(last_far, 64, 1))

            @pl.when(step != 0)
            def _():
                block_copy(step).start()

        return carry

    lax.fori_loop(0, devices // 2, send, 0)
    rbuf[0] = sbuf[0]

    def unfold(ref, start, end):
        rows = (end - start) * 8
        got = [ref[start:end, at : at + 8].reshape(rows, 128) for at in range(0, ROWS, 8)]
        return got[0::2], [got[1], got[3], pltpu.roll(got[4], 64, 1)]

    fetches[6].wait()
    fetches[7].wait()
    rows = devices * 8
    shape = (rows, 128)
    owner = me + lax.shift_right_logical(lax.broadcasted_iota(jnp.int32, shape, 0), 3)
    owner = jnp.where(owner >= devices, owner - devices, owner)
    powers = [power_ref[d : d + 1, :] for d in range(3)]
    lane_used = lax.broadcasted_iota(jnp.int32, shape, 1) < MONOS
    grown = jnp.zeros((128, 384), F32)
    for side in unfold(sbuf, 0, devices):
        leaf = jnp.broadcast_to(side[2][:, 63:64], shape)
        cell = owner * LEAF_DEV + leaf.astype(jnp.int32)
        factor = jnp.where((leaf >= 0.0) & lane_used, 1.0, 0.0)
        for d in range(3):
            bits = jnp.zeros(shape, jnp.int32)
            for j in range(depth[d]):
                moved = lax.shift_right_logical(cell, 2 * j + d) if 2 * j + d else cell
                bits = bits | (moved & (1 << j))
            centre = bits.astype(F32) * 2.0 ** (1 - depth[d]) - (1.0 - 2.0 ** -depth[d])
            for least in range(1, 5):
                factor = factor * jnp.where(powers[d] >= least, centre, 1.0)
        c_high, c_low = split(jnp.transpose(factor))
        high, low = split(jnp.concatenate(side, axis=1))
        grown = grown + dot(c_high, high, NN) + dot(c_low, high, NN) + dot(c_high, low, NN)
    sums = []
    for found in tile_places:
        total = None
        for i, j, at in found:
            term = grown[8 * i : 8 * i + 8, 128 * j : 128 * j + 128] * shift_ref[at]
            total = term if total is None else total + term
        sums.append(total)
    ones = jnp.ones((8, 128), F32)
    (tiles,) = gather_same([jnp.concatenate(sums, axis=0)], ones, spread_ref[1], lane8)
    own = jnp.concatenate(
        [jnp.sum(t, axis=0, keepdims=True) for t in tiles] + [jnp.zeros((1, 128), F32)], axis=0
    )
    root_send[...] = own

    def send_root(step, carry):
        root_copy(step).start()
        return carry

    lax.fori_loop(1, devices, send_root, 0)

    def take(step, carry):
        block_copy(step).wait()
        return carry

    cells = jnp.zeros((LEAF_DEV, 384), F32)
    bounds = [0, devices // 2, devices // 8 * 7, devices]
    for start, end in zip(bounds[:-1], bounds[1:]):
        lax.fori_loop(max(start, 1), end, take, 0)
        rows = (end - start) * 8
        leaf_lane = lax.broadcasted_iota(jnp.int32, (rows, 128), 1).astype(F32)
        for side in unfold(rbuf, start, end):
            hit = jnp.where(side[2][:, 63:64] == leaf_lane, 1.0, 0.0)
            hit = jnp.transpose(hit).astype(BF16)
            high, low = split(jnp.concatenate(side, axis=1))
            cells = cells + dot(hit, high, NN) + dot(hit, low, NN)
    fetches[5].wait()
    perm = perm_ref[...]
    high, low = split(cells)
    leaf_made[...] = (dot(perm, high, NT) + dot(perm, low, NT))[:COEFFS]
    leaf_store = pltpu.make_async_copy(leaf_made, leaf_out, out_sem.at[0])
    leaf_store.start()

    def take_root(step, carry):
        root_copy(step).wait()
        return carry

    lax.fori_loop(1, devices, take_root, 0)
    root_recv[0] = own
    total = jnp.sum(root_recv[...], axis=0)
    line = jnp.concatenate([total[0:1], total[1:2], total[2:3]], axis=1)
    high, low = split(jnp.broadcast_to(line, (16, 384)))
    root_made[...] = (dot(high, perm, NT) + dot(low, perm, NT))[0:1, :COEFFS]
    root_store = pltpu.make_async_copy(root_made, root_out, out_sem.at[1])
    root_store.start()
    leaf_store.wait()
    root_store.wait()


def hand_over(leaf_in, root_in, leaf_out, root_out, leaf_held, root_held, sem):
    incoming = [
        pltpu.make_async_copy(leaf_in, leaf_held, sem.at[0]),
        pltpu.make_async_copy(root_in, root_held, sem.at[1]),
    ]
    outgoing = [
        pltpu.make_async_copy(leaf_held, leaf_out, sem.at[2]),
        pltpu.make_async_copy(root_held, root_out, sem.at[3]),
    ]
    for copy in incoming:
        copy.start()
    for first, then in zip(incoming, outgoing):
        first.wait()
        then.start()
    for copy in outgoing:
        copy.wait()


def local(devices, low_size, segments, send_counts, send_offsets, leaf_of_block):
    blocks = segments.shape[0]
    levels = LEAF_DEV.bit_length() - 1 + devices.bit_length() - 1
    depth = [len(range(d, levels, 3)) for d in range(3)]
    shift_tiles, tile_places = make_shift_tiles(depth, 2.0 ** (-levels / 2))
    powers = np.zeros((8, 128), np.int32)
    powers[:3, :MONOS] = np.array(EXPONENTS).T
    lanes = np.arange(128)
    one = (lanes[None, :] % 9 == lanes[:, None] // 8) & (lanes[:, None] < 72)
    two = (lanes[None, :] % 9 == lanes[:, None] % 9) & (lanes[:, None] < 126)
    spread = np.stack([np.concatenate([x, x], axis=0) for x in (one, two)])
    spread = jnp.asarray(spread.astype(np.float32), BF16)
    perm = jnp.asarray(make_permutation(), BF16)
    hbm = pl.BlockSpec(memory_space=pltpu.HBM)
    dma = pltpu.SemaphoreType.DMA
    shapes = (
        jax.ShapeDtypeStruct((COEFFS, LEAF_DEV), F32),
        jax.ShapeDtypeStruct((1, COEFFS), F32),
    )
    results = pl.pallas_call(
        functools.partial(kernel, devices, low_size, depth, tile_places),
        out_shape=shapes,
        in_specs=[hbm] * 8,
        out_specs=(hbm, hbm),
        scratch_shapes=[
            pltpu.VMEM((9, blocks + SLOTS, 128), F32),
            pltpu.VMEM((blocks // 128, 128), jnp.int32),
            pltpu.VMEM((320, 384), BF16),
            pltpu.VMEM((2, 256, 128), BF16),
            pltpu.SMEM((1, devices), jnp.int32),
            pltpu.SMEM((1, devices), jnp.int32),
            pltpu.VMEM(shift_tiles.shape, F32),
            pltpu.VMEM(powers.shape, jnp.int32),
            pltpu.VMEM((blocks + SLOTS, 128), F32),
            pltpu.VMEM((devices, ROWS, 128), F32),
            pltpu.VMEM((devices, ROWS, 128), F32),
            pltpu.VMEM((4, 128), F32),
            pltpu.VMEM((devices, 4, 128), F32),
            pltpu.VMEM((COEFFS, LEAF_DEV), F32),
            pltpu.VMEM((1, COEFFS), F32),
            dma((8,)),
            dma((devices,)),
            dma((devices,)),
            dma((devices,)),
            dma((devices,)),
            dma((2,)),
        ],
        compiler_params=pltpu.CompilerParams(
            collective_id=0, has_side_effects=True, vmem_limit_bytes=63 * 1024 * 1024
        ),
        cost_estimate=pl.CostEstimate(
            flops=2 * blocks * 128 * COEFFS * 2, bytes_accessed=blocks * 128 * 40, transcendentals=0
        ),
    )(
        jnp.transpose(segments, (1, 0, 2)),
        leaf_of_block.reshape(blocks // 128, 128),
        perm,
        spread,
        send_counts,
        send_offsets,
        jnp.asarray(shift_tiles),
        jnp.asarray(powers),
    )
    return pl.pallas_call(
        hand_over,
        out_shape=shapes,
        in_specs=[hbm, hbm],
        out_specs=(hbm, hbm),
        scratch_shapes=[
            pltpu.VMEM((COEFFS, LEAF_DEV), F32),
            pltpu.VMEM((1, COEFFS), F32),
            dma((4,)),
        ],
        compiler_params=pltpu.CompilerParams(vmem_limit_bytes=63 * 1024 * 1024),
    )(*results)


def solution(mesh):
    placed = (
        P(("top", "low"), None, None),
        P(("top", "low"), None),
        P(("top", "low"), None),
        P(("top", "low")),
    )
    return jax.shard_map(
        functools.partial(local, mesh.size, mesh.shape["low"]),
        mesh=mesh,
        in_specs=placed,
        out_specs=(P(None, ("top", "low")), P(("top", "low"), None)),
        check_vma=False,
    )
```

```python
import functools
import math

import jax
import jax.numpy as jnp
import numpy as np
from jax import lax
from jax.experimental import pallas as pl
from jax.experimental.pallas import tpu as pltpu
from jax.sharding import PartitionSpec as P

MONOS = 35
COEFFS = 315
LEAF_DEV = 128
SLOTS = 16
ROWS = 2 * SLOTS + SLOTS // 2
MESH = pl.DeviceIdType.MESH
BF16 = jnp.bfloat16
F32 = jnp.float32
NT = (((1,), (1,)), ((), ()))
NN = (((1,), (0,)), ((), ()))


def make_exponents():
    collected = []
    for degree_total in range(5):
        for first_power in range(degree_total, -1, -1):
            for second_power in range(degree_total - first_power, -1, -1):
                collected.append(
                    (first_power, second_power, degree_total - first_power - second_power)
                )
    return collected


EXPONENTS = make_exponents()
POINTS = (
    (-math.sqrt(0.6), 5.0 / 18.0),
    (0.0, 8.0 / 18.0),
    (math.sqrt(0.6), 5.0 / 18.0),
)


def make_permutation():
    table = np.zeros((320, 384), np.float32)
    for m in range(MONOS):
        for a in range(9):
            table[MONOS * a + m, 128 * (m // 14) + 9 * (m % 14) + a] = 1.0
    return table


def make_shift_tiles(depth, scale):
    tiles, places = [], []
    for target in EXPONENTS:
        table = np.zeros((40, 384), np.float32)
        for n, source in enumerate(EXPONENTS):
            rest = tuple(t - s for t, s in zip(target, source))
            if min(rest) < 0:
                continue
            factor = scale
            for t, s, d in zip(target, source, depth):
                factor *= math.comb(t, s) * 2.0 ** (-d * s)
            lane = 128 * (n // 14) + 9 * (n % 14)
            table[EXPONENTS.index(rest), lane : lane + 9] = factor
        found = []
        for i in range(5):
            for j in range(3):
                tile = table[8 * i : 8 * i + 8, 128 * j : 128 * j + 128]
                if tile.any():
                    found.append((i, j, len(tiles)))
                    tiles.append(tile)
        places.append(found)
    return np.stack(tiles), places


def split(x):
    high = x.astype(BF16)
    low = (x - high.astype(F32)).astype(BF16)
    return high, low


def dot(a, b, dims):
    return lax.dot_general(a, b, dims, preferred_element_type=F32)


def monomials(middle, half):
    total = None
    for point, weight in POINTS:
        at = [m + point * h if point else m for m, h in zip(middle, half)]
        made = {(0, 0, 0): None}
        values = []
        for e in EXPONENTS[1:]:
            axis = next(i for i in range(3) if e[i] > 0)
            lower = tuple(p - (i == axis) for i, p in enumerate(e))
            before = made[lower]
            made[e] = at[axis] * weight if before is None else before * at[axis]
            values.append(made[e])
        total = values if total is None else [x + y for x, y in zip(total, values)]
    return [jnp.ones_like(middle[0])] + total


def pair_products(quads, tensors):
    q_high, q_low = split(jnp.concatenate(quads, axis=0))
    stacked = jnp.concatenate(tensors + [jnp.zeros((56, 128), F32)], axis=0)
    right = jnp.concatenate(split(jnp.transpose(stacked)), axis=1)
    left = jnp.concatenate([q_high, q_low], axis=1)
    both = dot(left, jnp.concatenate([right, right], axis=0), NN)
    return both[:, :128] + both[:, 128:]


def lay_out(pieces, lane):
    tiles = []
    for first in (0, 14, 28):
        tile = jnp.zeros((8, 128), F32)
        for k in reversed(range(min(14, MONOS - first))):
            tile = jnp.where(lane < 9 * k + 9, pieces[first + k], tile)
        tiles.append(tile)
    return tiles


def pick_same(products, index, lane):
    pieces = [
        jnp.take_along_axis(
            products[8 * m : 8 * m + 8], index, axis=1, mode="promise_in_bounds"
        )
        for m in range(MONOS)
    ]
    return lay_out(pieces, lane)


def column(row):
    return jnp.transpose(jnp.broadcast_to(row, (128, 128)))


def kernel(
    devices, low_size, depth, tile_places,
    seg_hbm, leaf_hbm, perm_hbm, spread_hbm, count_hbm, offset_hbm, shift_hbm, power_hbm,
    leaf_out, root_out,
    seg_ref, leaf_ref, perm_ref, spread_ref, count_ref, offset_ref, shift_ref, power_ref,
    place, sbuf, rbuf, root_send, root_recv,
    leaf_made, root_made,
    load_sem, send_sem, recv_sem, root_send_sem, root_recv_sem, out_sem,
):
    blocks = seg_ref.shape[1] - SLOTS
    body_rows = pl.ds(0, blocks)
    fetches = [
        pltpu.make_async_copy(src, dst, load_sem.at[i])
        for i, (src, dst) in enumerate(
            (
                (leaf_hbm, leaf_ref),
                (seg_hbm, seg_ref.at[:, body_rows]),
                (spread_hbm, spread_ref),
                (count_hbm, count_ref),
                (offset_hbm, offset_ref),
                (perm_hbm, perm_ref),
                (shift_hbm, shift_ref),
                (power_hbm, power_ref),
            )
        )
    ]
    for fetch in fetches:
        fetch.start()

    me = lax.axis_index("top") * low_size + lax.axis_index("low")

    def partner(step):
        other = lax.rem(me + step, devices)
        return other, (other // low_size, lax.rem(other, low_size))

    barrier = pltpu.get_barrier_semaphore()

    def greet(step, carry):
        pl.semaphore_signal(barrier, inc=1, device_id=partner(step)[1], device_id_type=MESH)
        return carry

    lax.fori_loop(1, devices, greet, 0)
    seg_ref[:, blocks:] = jnp.zeros((9, SLOTS, 128), F32)
    place[blocks:] = jnp.zeros((SLOTS, 128), F32)

    fetches[0].wait()
    leaves = leaf_ref[...]
    for chunk in range(blocks // 128):
        place[chunk * 128 : chunk * 128 + 128] = column(
            leaves[chunk : chunk + 1].astype(F32)
        )
    for fetch in fetches[1:5]:
        fetch.wait()

    lane8 = lax.broadcasted_iota(jnp.int32, (8, 128), 1)
    row8 = lax.broadcasted_iota(jnp.int32, (8, 128), 0)
    same = 8 * lax.rem(lane8, 9) + row8

    def load(rows):
        parts = [seg_ref[c, rows, :] for c in range(9)]
        scaled = [h * (2.0 / math.sqrt(128.0)) for h in parts[6:9]]
        tensors = [b * h for b in parts[0:3] for h in scaled]
        return parts[3:6], parts[6:9], tensors

    def block_copy(step):
        return pltpu.make_async_remote_copy(
            src_ref=sbuf.at[step], dst_ref=rbuf.at[step],
            send_sem=send_sem.at[step], recv_sem=recv_sem.at[step],
            device_id=partner(step)[1], device_id_type=MESH,
        )

    def root_copy(step):
        return pltpu.make_async_remote_copy(
            src_ref=root_send, dst_ref=root_recv.at[step],
            send_sem=root_send_sem.at[step], recv_sem=root_recv_sem.at[step],
            device_id=partner(step)[1], device_id_type=MESH,
        )

    pl.semaphore_wait(barrier, devices - 1)

    def send(turn, carry):
        steps, products, leaf_rows = [], [], []
        for u in range(2):
            step = lax.rem(turn * 2 + u + 1, devices)
            owner = partner(step)[0]
            for side in (0, 8):
                rows = pl.ds(offset_ref[0, owner] + side, 8)
                middle, half, tensors = load(rows)
                products.append(pair_products(monomials(middle, half), tensors))
                leaf = jnp.where(row8 + side < count_ref[0, owner], place[rows, :], -1.0)
                leaf_rows.append(leaf)
            steps.append(step)
        made = [pick_same(one, same, lane8) for one in products]
        for u, step in enumerate(steps):
            near, far = made[2 * u : 2 * u + 2]
            last_near = jnp.where(lane8 == 63, leaf_rows[2 * u], near[2])
            last_far = jnp.where(lane8 == 63, leaf_rows[2 * u + 1], far[2])
            sbuf[step, 0:8, :] = near[0]
            sbuf[step, 8:16, :] = far[0]
            sbuf[step, 16:24, :] = near[1]
            sbuf[step, 24:32, :] = far[1]
            sbuf[step, 32:40, :] = jnp.where(lane8 < 64, last_near, pltpu.roll(last_far, 64, 1))

            @pl.when(step != 0)
            def _():
                block_copy(step).start()

        return carry

    lax.fori_loop(0, devices // 2, send, 0)
    rbuf[0] = sbuf[0]

    def unfold(ref, start, end):
        rows = (end - start) * 8
        got = [ref[start:end, at : at + 8].reshape(rows, 128) for at in range(0, ROWS, 8)]
        return got[0::2], [got[1], got[3], pltpu.roll(got[4], 64, 1)]

    fetches[6].wait()
    fetches[7].wait()
    rows = devices * 8
    shape = (rows, 128)
    owner = me + lax.shift_right_logical(lax.broadcasted_iota(jnp.int32, shape, 0), 3)
    owner = jnp.where(owner >= devices, owner - devices, owner)
    powers = [power_ref[d : d + 1, :] for d in range(3)]
    lane_used = lax.broadcasted_iota(jnp.int32, shape, 1) < MONOS
    grown = jnp.zeros((128, 384), F32)
    for side in unfold(sbuf, 0, devices):
        leaf = jnp.broadcast_to(side[2][:, 63:64], shape)
        cell = owner * LEAF_DEV + leaf.astype(jnp.int32)
        factor = jnp.where((leaf >= 0.0) & lane_used, 1.0, 0.0)
        for d in range(3):
            bits = jnp.zeros(shape, jnp.int32)
            for j in range(depth[d]):
                moved = lax.shift_right_logical(cell, 2 * j + d) if 2 * j + d else cell
                bits = bits | (moved & (1 << j))
            centre = bits.astype(F32) * 2.0 ** (1 - depth[d]) - (1.0 - 2.0 ** -depth[d])
            for least in range(1, 5):
                factor = factor * jnp.where(powers[d] >= least, centre, 1.0)
        c_high, c_low = split(jnp.transpose(factor))
        high, low = split(jnp.concatenate(side, axis=1))
        grown = grown + dot(c_high, high, NN) + dot(c_low, high, NN) + dot(c_high, low, NN)
    sums = []
    for found in tile_places:
        total = None
        for i, j, at in found:
            term = grown[8 * i : 8 * i + 8, 128 * j : 128 * j + 128] * shift_ref[at]
            total = term if total is None else total + term
        sums.append(total)
    sums = jnp.concatenate(split(jnp.concatenate(sums, axis=0)), axis=1)
    sums = dot(sums, spread_ref[...], NN)
    tiles = lay_out([sums[8 * m : 8 * m + 8] for m in range(MONOS)], lane8)
    own = jnp.concatenate(
        [jnp.sum(t, axis=0, keepdims=True) for t in tiles] + [jnp.zeros((1, 128), F32)], axis=0
    )
    root_send[...] = own

    def send_root(step, carry):
        root_copy(step).start()
        return carry

    lax.fori_loop(1, devices, send_root, 0)

    def take(step, carry):
        block_copy(step).wait()
        return carry

    cells = jnp.zeros((LEAF_DEV, 384), F32)
    bounds = [0, devices // 2, devices // 8 * 7, devices]
    for start, end in zip(bounds[:-1], bounds[1:]):
        lax.fori_loop(max(start, 1), end, take, 0)
        rows = (end - start) * 8
        leaf_lane = lax.broadcasted_iota(jnp.int32, (rows, 128), 1).astype(F32)
        for side in unfold(rbuf, start, end):
            hit = jnp.where(side[2][:, 63:64] == leaf_lane, 1.0, 0.0)
            hit = jnp.transpose(hit).astype(BF16)
            high, low = split(jnp.concatenate(side, axis=1))
            cells = cells + dot(hit, high, NN) + dot(hit, low, NN)
    fetches[5].wait()
    perm = perm_ref[...]
    high, low = split(cells)
    leaf_made[...] = (dot(perm, high, NT) + dot(perm, low, NT))[:COEFFS]
    leaf_store = pltpu.make_async_copy(leaf_made, leaf_out, out_sem.at[0])
    leaf_store.start()

    def take_root(step, carry):
        root_copy(step).wait()
        return carry

    lax.fori_loop(1, devices, take_root, 0)
    root_recv[0] = own
    total = jnp.sum(root_recv[...], axis=0)
    line = jnp.concatenate([total[0:1], total[1:2], total[2:3]], axis=1)
    high, low = split(jnp.broadcast_to(line, (16, 384)))
    root_made[...] = (dot(high, perm, NT) + dot(low, perm, NT))[0:1, :COEFFS]
    root_store = pltpu.make_async_copy(root_made, root_out, out_sem.at[1])
    root_store.start()
    leaf_store.wait()
    root_store.wait()


def hand_over(leaf_in, root_in, leaf_out, root_out, leaf_held, root_held, sem):
    incoming = [
        pltpu.make_async_copy(leaf_in, leaf_held, sem.at[0]),
        pltpu.make_async_copy(root_in, root_held, sem.at[1]),
    ]
    outgoing = [
        pltpu.make_async_copy(leaf_held, leaf_out, sem.at[2]),
        pltpu.make_async_copy(root_held, root_out, sem.at[3]),
    ]
    for copy in incoming:
        copy.start()
    for first, then in zip(incoming, outgoing):
        first.wait()
        then.start()
    for copy in outgoing:
        copy.wait()


def local(devices, low_size, segments, send_counts, send_offsets, leaf_of_block):
    blocks = segments.shape[0]
    levels = LEAF_DEV.bit_length() - 1 + devices.bit_length() - 1
    depth = [len(range(d, levels, 3)) for d in range(3)]
    shift_tiles, tile_places = make_shift_tiles(depth, 2.0 ** (-levels / 2))
    powers = np.zeros((8, 128), np.int32)
    powers[:3, :MONOS] = np.array(EXPONENTS).T
    lanes = np.arange(128)
    spread = (lanes[None, :] % 9 == lanes[:, None] % 9) & (lanes[:, None] < 126)
    spread = np.concatenate([spread, spread], axis=0).astype(np.float32)
    spread = jnp.asarray(spread, BF16)
    perm = jnp.asarray(make_permutation(), BF16)
    hbm = pl.BlockSpec(memory_space=pltpu.HBM)
    dma = pltpu.SemaphoreType.DMA
    shapes = (
        jax.ShapeDtypeStruct((COEFFS, LEAF_DEV), F32),
        jax.ShapeDtypeStruct((1, COEFFS), F32),
    )
    results = pl.pallas_call(
        functools.partial(kernel, devices, low_size, depth, tile_places),
        out_shape=shapes,
        in_specs=[hbm] * 8,
        out_specs=(hbm, hbm),
        scratch_shapes=[
            pltpu.VMEM((9, blocks + SLOTS, 128), F32),
            pltpu.VMEM((blocks // 128, 128), jnp.int32),
            pltpu.VMEM((320, 384), BF16),
            pltpu.VMEM((256, 128), BF16),
            pltpu.SMEM((1, devices), jnp.int32),
            pltpu.SMEM((1, devices), jnp.int32),
            pltpu.VMEM(shift_tiles.shape, F32),
            pltpu.VMEM(powers.shape, jnp.int32),
            pltpu.VMEM((blocks + SLOTS, 128), F32),
            pltpu.VMEM((devices, ROWS, 128), F32),
            pltpu.VMEM((devices, ROWS, 128), F32),
            pltpu.VMEM((4, 128), F32),
            pltpu.VMEM((devices, 4, 128), F32),
            pltpu.VMEM((COEFFS, LEAF_DEV), F32),
            pltpu.VMEM((1, COEFFS), F32),
            dma((8,)),
            dma((devices,)),
            dma((devices,)),
            dma((devices,)),
            dma((devices,)),
            dma((2,)),
        ],
        compiler_params=pltpu.CompilerParams(
            collective_id=0, has_side_effects=True, vmem_limit_bytes=63 * 1024 * 1024
        ),
        cost_estimate=pl.CostEstimate(
            flops=2 * blocks * 128 * COEFFS * 2, bytes_accessed=blocks * 128 * 40, transcendentals=0
        ),
    )(
        jnp.transpose(segments, (1, 0, 2)),
        leaf_of_block.reshape(blocks // 128, 128),
        perm,
        spread,
        send_counts,
        send_offsets,
        jnp.asarray(shift_tiles),
        jnp.asarray(powers),
    )
    return pl.pallas_call(
        hand_over,
        out_shape=shapes,
        in_specs=[hbm, hbm],
        out_specs=(hbm, hbm),
        scratch_shapes=[
            pltpu.VMEM((COEFFS, LEAF_DEV), F32),
            pltpu.VMEM((1, COEFFS), F32),
            dma((4,)),
        ],
        compiler_params=pltpu.CompilerParams(vmem_limit_bytes=63 * 1024 * 1024),
    )(*results)


def solution(mesh):
    placed = (
        P(("top", "low"), None, None),
        P(("top", "low"), None),
        P(("top", "low"), None),
        P(("top", "low")),
    )
    return jax.shard_map(
        functools.partial(local, mesh.size, mesh.shape["low"]),
        mesh=mesh,
        in_specs=placed,
        out_specs=(P(None, ("top", "low")), P(("top", "low"), None)),
        check_vma=False,
    )
```

```python
import functools
import math

import jax
import jax.numpy as jnp
import numpy as np
from jax import lax
from jax.experimental import pallas as pl
from jax.experimental.pallas import tpu as pltpu
from jax.sharding import PartitionSpec as P

MONOS = 35
COEFFS = 315
LEAF_DEV = 128
SLOTS = 16
ROWS = 2 * SLOTS + SLOTS // 2
MESH = pl.DeviceIdType.MESH
BF16 = jnp.bfloat16
F32 = jnp.float32
NT = (((1,), (1,)), ((), ()))
NN = (((1,), (0,)), ((), ()))


def make_exponents():
    collected = []
    for degree_total in range(5):
        for first_power in range(degree_total, -1, -1):
            for second_power in range(degree_total - first_power, -1, -1):
                collected.append(
                    (first_power, second_power, degree_total - first_power - second_power)
                )
    return collected


EXPONENTS = make_exponents()
POINTS = (
    (-math.sqrt(0.6), 5.0 / 18.0),
    (0.0, 8.0 / 18.0),
    (math.sqrt(0.6), 5.0 / 18.0),
)


def make_permutation():
    table = np.zeros((320, 384), np.float32)
    for m in range(MONOS):
        for a in range(9):
            table[MONOS * a + m, 128 * (m // 14) + 9 * (m % 14) + a] = 1.0
    return table


def make_shift_tiles(depth, scale):
    tiles, places = [], []
    for target in EXPONENTS:
        table = np.zeros((40, 384), np.float32)
        for n, source in enumerate(EXPONENTS):
            rest = tuple(t - s for t, s in zip(target, source))
            if min(rest) < 0:
                continue
            factor = scale
            for t, s, d in zip(target, source, depth):
                factor *= math.comb(t, s) * 2.0 ** (-d * s)
            lane = 128 * (n // 14) + 9 * (n % 14)
            table[EXPONENTS.index(rest), lane : lane + 9] = factor
        found = []
        for i in range(5):
            for j in range(3):
                tile = table[8 * i : 8 * i + 8, 128 * j : 128 * j + 128]
                if tile.any():
                    found.append((i, j, len(tiles)))
                    tiles.append(tile)
        places.append(found)
    return np.stack(tiles), places


def split(x):
    high = x.astype(BF16)
    low = (x - high.astype(F32)).astype(BF16)
    return high, low


def dot(a, b, dims):
    return lax.dot_general(a, b, dims, preferred_element_type=F32)


def monomials(middle, half):
    total = None
    for point, weight in POINTS:
        at = [m + point * h if point else m for m, h in zip(middle, half)]
        made = {(0, 0, 0): None}
        values = []
        for e in EXPONENTS[1:]:
            axis = next(i for i in range(3) if e[i] > 0)
            lower = tuple(p - (i == axis) for i, p in enumerate(e))
            before = made[lower]
            made[e] = at[axis] * weight if before is None else before * at[axis]
            values.append(made[e])
        total = values if total is None else [x + y for x, y in zip(total, values)]
    return [jnp.ones_like(middle[0])] + total


def pair_products(quads, tensors):
    q_high, q_low = split(jnp.concatenate(quads, axis=0))
    stacked = jnp.concatenate(tensors + [jnp.zeros((56, 128), F32)], axis=0)
    right = jnp.concatenate(split(jnp.transpose(stacked)), axis=1)
    left = jnp.concatenate([q_high, q_low], axis=1)
    both = dot(left, jnp.concatenate([right, right], axis=0), NN)
    return both[:, :128] + both[:, 128:]


def lay_out(pieces, lane):
    tiles = []
    for first in (0, 14, 28):
        tile = jnp.zeros((8, 128), F32)
        for k in reversed(range(min(14, MONOS - first))):
            tile = jnp.where(lane < 9 * k + 9, pieces[first + k], tile)
        tiles.append(tile)
    return tiles


def pick_same(products, index, lane):
    pieces = [
        jnp.take_along_axis(
            products[8 * m : 8 * m + 8], index, axis=1, mode="promise_in_bounds"
        )
        for m in range(MONOS)
    ]
    return lay_out(pieces, lane)


def column(row):
    return jnp.transpose(jnp.broadcast_to(row, (128, 128)))


def kernel(
    devices, low_size, depth, tile_places,
    seg_hbm, leaf_hbm, perm_hbm, spread_hbm, count_hbm, offset_hbm, shift_hbm, power_hbm,
    leaf_out, root_out,
    seg_ref, leaf_ref, perm_ref, spread_ref, count_ref, offset_ref, shift_ref, power_ref,
    place, sbuf, rbuf, root_send, top_recv, low_recv,
    leaf_made, root_made,
    load_sem, send_sem, recv_sem, top_send_sem, top_recv_sem, low_send_sem, low_recv_sem, out_sem,
):
    blocks = seg_ref.shape[1] - SLOTS
    body_rows = pl.ds(0, blocks)
    fetches = [
        pltpu.make_async_copy(src, dst, load_sem.at[i])
        for i, (src, dst) in enumerate(
            (
                (leaf_hbm, leaf_ref),
                (seg_hbm, seg_ref.at[:, body_rows]),
                (spread_hbm, spread_ref),
                (count_hbm, count_ref),
                (offset_hbm, offset_ref),
                (perm_hbm, perm_ref),
                (shift_hbm, shift_ref),
                (power_hbm, power_ref),
            )
        )
    ]
    for fetch in fetches:
        fetch.start()

    me = lax.axis_index("top") * low_size + lax.axis_index("low")

    def partner(step):
        other = lax.rem(me + step, devices)
        return other, (other // low_size, lax.rem(other, low_size))

    barrier = pltpu.get_barrier_semaphore()

    def greet(step, carry):
        pl.semaphore_signal(barrier, inc=1, device_id=partner(step)[1], device_id_type=MESH)
        return carry

    lax.fori_loop(1, devices, greet, 0)
    seg_ref[:, blocks:] = jnp.zeros((9, SLOTS, 128), F32)
    place[blocks:] = jnp.zeros((SLOTS, 128), F32)

    fetches[0].wait()
    leaves = leaf_ref[...]
    for chunk in range(blocks // 128):
        place[chunk * 128 : chunk * 128 + 128] = column(
            leaves[chunk : chunk + 1].astype(F32)
        )
    for fetch in fetches[1:5]:
        fetch.wait()

    lane8 = lax.broadcasted_iota(jnp.int32, (8, 128), 1)
    row8 = lax.broadcasted_iota(jnp.int32, (8, 128), 0)
    same = 8 * lax.rem(lane8, 9) + row8

    def load(rows):
        parts = [seg_ref[c, rows, :] for c in range(9)]
        scaled = [h * (2.0 / math.sqrt(128.0)) for h in parts[6:9]]
        tensors = [b * h for b in parts[0:3] for h in scaled]
        return parts[3:6], parts[6:9], tensors

    def block_copy(step):
        return pltpu.make_async_remote_copy(
            src_ref=sbuf.at[step], dst_ref=rbuf.at[step],
            send_sem=send_sem.at[step], recv_sem=recv_sem.at[step],
            device_id=partner(step)[1], device_id_type=MESH,
        )

    my_top, my_low = lax.axis_index("top"), lax.axis_index("low")
    top_size = devices // low_size

    def top_copy(step):
        return pltpu.make_async_remote_copy(
            src_ref=root_send.at[0], dst_ref=top_recv.at[step],
            send_sem=top_send_sem.at[step], recv_sem=top_recv_sem.at[step],
            device_id=(lax.rem(my_top + step, top_size), my_low), device_id_type=MESH,
        )

    def low_copy(step):
        return pltpu.make_async_remote_copy(
            src_ref=root_send.at[1], dst_ref=low_recv.at[step],
            send_sem=low_send_sem.at[step], recv_sem=low_recv_sem.at[step],
            device_id=(my_top, lax.rem(my_low + step, low_size)), device_id_type=MESH,
        )

    def start_all(copy, count):
        def body(step, carry):
            copy(step).start()
            return carry

        lax.fori_loop(1, count, body, 0)

    def wait_all(copy, count):
        def body(step, carry):
            copy(step).wait()
            return carry

        lax.fori_loop(1, count, body, 0)

    pl.semaphore_wait(barrier, devices - 1)

    def send(turn, carry):
        steps, products, leaf_rows = [], [], []
        for u in range(2):
            step = lax.rem(turn * 2 + u + 1, devices)
            owner = partner(step)[0]
            for side in (0, 8):
                rows = pl.ds(offset_ref[0, owner] + side, 8)
                middle, half, tensors = load(rows)
                products.append(pair_products(monomials(middle, half), tensors))
                leaf = jnp.where(row8 + side < count_ref[0, owner], place[rows, :], -1.0)
                leaf_rows.append(leaf)
            steps.append(step)
        made = [pick_same(one, same, lane8) for one in products]
        for u, step in enumerate(steps):
            near, far = made[2 * u : 2 * u + 2]
            last_near = jnp.where(lane8 == 63, leaf_rows[2 * u], near[2])
            last_far = jnp.where(lane8 == 63, leaf_rows[2 * u + 1], far[2])
            sbuf[step, 0:8, :] = near[0]
            sbuf[step, 8:16, :] = far[0]
            sbuf[step, 16:24, :] = near[1]
            sbuf[step, 24:32, :] = far[1]
            sbuf[step, 32:40, :] = jnp.where(lane8 < 64, last_near, pltpu.roll(last_far, 64, 1))

            @pl.when(step != 0)
            def _():
                block_copy(step).start()

        return carry

    lax.fori_loop(0, devices // 2, send, 0)
    rbuf[0] = sbuf[0]

    def unfold(ref, start, end):
        rows = (end - start) * 8
        got = [ref[start:end, at : at + 8].reshape(rows, 128) for at in range(0, ROWS, 8)]
        return got[0::2], [got[1], got[3], pltpu.roll(got[4], 64, 1)]

    fetches[6].wait()
    fetches[7].wait()
    rows = devices * 8
    shape = (rows, 128)
    owner = me + lax.shift_right_logical(lax.broadcasted_iota(jnp.int32, shape, 0), 3)
    owner = jnp.where(owner >= devices, owner - devices, owner)
    powers = [power_ref[d : d + 1, :] for d in range(3)]
    lane_used = lax.broadcasted_iota(jnp.int32, shape, 1) < MONOS
    grown = jnp.zeros((128, 384), F32)
    for side in unfold(sbuf, 0, devices):
        leaf = jnp.broadcast_to(side[2][:, 63:64], shape)
        cell = owner * LEAF_DEV + leaf.astype(jnp.int32)
        factor = jnp.where((leaf >= 0.0) & lane_used, 1.0, 0.0)
        for d in range(3):
            bits = jnp.zeros(shape, jnp.int32)
            for j in range(depth[d]):
                moved = lax.shift_right_logical(cell, 2 * j + d) if 2 * j + d else cell
                bits = bits | (moved & (1 << j))
            centre = bits.astype(F32) * 2.0 ** (1 - depth[d]) - (1.0 - 2.0 ** -depth[d])
            for least in range(1, 5):
                factor = factor * jnp.where(powers[d] >= least, centre, 1.0)
        c_high, c_low = split(jnp.transpose(factor))
        high, low = split(jnp.concatenate(side, axis=1))
        grown = grown + dot(c_high, high, NN) + dot(c_low, high, NN) + dot(c_high, low, NN)
    sums = []
    for found in tile_places:
        total = None
        for i, j, at in found:
            term = grown[8 * i : 8 * i + 8, 128 * j : 128 * j + 128] * shift_ref[at]
            total = term if total is None else total + term
        sums.append(total)
    sums = jnp.concatenate(split(jnp.concatenate(sums, axis=0)), axis=1)
    sums = dot(sums, spread_ref[...], NN)
    tiles = lay_out([sums[8 * m : 8 * m + 8] for m in range(MONOS)], lane8)
    own = jnp.concatenate(
        [jnp.sum(t, axis=0, keepdims=True) for t in tiles] + [jnp.zeros((1, 128), F32)], axis=0
    )
    root_send[0] = own
    start_all(top_copy, top_size)

    def take(step, carry):
        block_copy(step).wait()
        return carry

    cells = jnp.zeros((LEAF_DEV, 384), F32)
    bounds = [0, devices // 2, devices // 4 * 3, devices // 8 * 7, devices]
    for start, end in zip(bounds[:-1], bounds[1:]):
        lax.fori_loop(max(start, 1), end, take, 0)
        if end == bounds[2]:
            wait_all(top_copy, top_size)
            top_recv[0] = own
            root_send[1] = jnp.sum(top_recv[...], axis=0)
            start_all(low_copy, low_size)
        rows = (end - start) * 8
        leaf_lane = lax.broadcasted_iota(jnp.int32, (rows, 128), 1).astype(F32)
        for side in unfold(rbuf, start, end):
            hit = jnp.where(side[2][:, 63:64] == leaf_lane, 1.0, 0.0)
            hit = jnp.transpose(hit).astype(BF16)
            high, low = split(jnp.concatenate(side, axis=1))
            cells = cells + dot(hit, high, NN) + dot(hit, low, NN)
    fetches[5].wait()
    perm = perm_ref[...]
    high, low = split(cells)
    leaf_made[...] = (dot(perm, high, NT) + dot(perm, low, NT))[:COEFFS]
    leaf_store = pltpu.make_async_copy(leaf_made, leaf_out, out_sem.at[0])
    leaf_store.start()

    wait_all(low_copy, low_size)
    low_recv[0] = root_send[1]
    total = jnp.sum(low_recv[...], axis=0)
    line = jnp.concatenate([total[0:1], total[1:2], total[2:3]], axis=1)
    high, low = split(jnp.broadcast_to(line, (16, 384)))
    root_made[...] = (dot(high, perm, NT) + dot(low, perm, NT))[0:1, :COEFFS]
    root_store = pltpu.make_async_copy(root_made, root_out, out_sem.at[1])
    root_store.start()
    leaf_store.wait()
    root_store.wait()


def hand_over(leaf_in, root_in, leaf_out, root_out, leaf_held, root_held, sem):
    incoming = [
        pltpu.make_async_copy(leaf_in, leaf_held, sem.at[0]),
        pltpu.make_async_copy(root_in, root_held, sem.at[1]),
    ]
    outgoing = [
        pltpu.make_async_copy(leaf_held, leaf_out, sem.at[2]),
        pltpu.make_async_copy(root_held, root_out, sem.at[3]),
    ]
    for copy in incoming:
        copy.start()
    for first, then in zip(incoming, outgoing):
        first.wait()
        then.start()
    for copy in outgoing:
        copy.wait()


def local(devices, low_size, segments, send_counts, send_offsets, leaf_of_block):
    blocks = segments.shape[0]
    levels = LEAF_DEV.bit_length() - 1 + devices.bit_length() - 1
    depth = [len(range(d, levels, 3)) for d in range(3)]
    shift_tiles, tile_places = make_shift_tiles(depth, 2.0 ** (-levels / 2))
    powers = np.zeros((8, 128), np.int32)
    powers[:3, :MONOS] = np.array(EXPONENTS).T
    lanes = np.arange(128)
    spread = (lanes[None, :] % 9 == lanes[:, None] % 9) & (lanes[:, None] < 126)
    spread = np.concatenate([spread, spread], axis=0).astype(np.float32)
    spread = jnp.asarray(spread, BF16)
    perm = jnp.asarray(make_permutation(), BF16)
    hbm = pl.BlockSpec(memory_space=pltpu.HBM)
    dma = pltpu.SemaphoreType.DMA
    shapes = (
        jax.ShapeDtypeStruct((COEFFS, LEAF_DEV), F32),
        jax.ShapeDtypeStruct((1, COEFFS), F32),
    )
    results = pl.pallas_call(
        functools.partial(kernel, devices, low_size, depth, tile_places),
        out_shape=shapes,
        in_specs=[hbm] * 8,
        out_specs=(hbm, hbm),
        scratch_shapes=[
            pltpu.VMEM((9, blocks + SLOTS, 128), F32),
            pltpu.VMEM((blocks // 128, 128), jnp.int32),
            pltpu.VMEM((320, 384), BF16),
            pltpu.VMEM((256, 128), BF16),
            pltpu.SMEM((1, devices), jnp.int32),
            pltpu.SMEM((1, devices), jnp.int32),
            pltpu.VMEM(shift_tiles.shape, F32),
            pltpu.VMEM(powers.shape, jnp.int32),
            pltpu.VMEM((blocks + SLOTS, 128), F32),
            pltpu.VMEM((devices, ROWS, 128), F32),
            pltpu.VMEM((devices, ROWS, 128), F32),
            pltpu.VMEM((2, 4, 128), F32),
            pltpu.VMEM((devices // low_size, 4, 128), F32),
            pltpu.VMEM((low_size, 4, 128), F32),
            pltpu.VMEM((COEFFS, LEAF_DEV), F32),
            pltpu.VMEM((1, COEFFS), F32),
            dma((8,)),
            dma((devices,)),
            dma((devices,)),
            dma((devices // low_size,)),
            dma((devices // low_size,)),
            dma((low_size,)),
            dma((low_size,)),
            dma((2,)),
        ],
        compiler_params=pltpu.CompilerParams(
            collective_id=0, has_side_effects=True, vmem_limit_bytes=63 * 1024 * 1024
        ),
        cost_estimate=pl.CostEstimate(
            flops=2 * blocks * 128 * COEFFS * 2, bytes_accessed=blocks * 128 * 40, transcendentals=0
        ),
    )(
        jnp.transpose(segments, (1, 0, 2)),
        leaf_of_block.reshape(blocks // 128, 128),
        perm,
        spread,
        send_counts,
        send_offsets,
        jnp.asarray(shift_tiles),
        jnp.asarray(powers),
    )
    return pl.pallas_call(
        hand_over,
        out_shape=shapes,
        in_specs=[hbm, hbm],
        out_specs=(hbm, hbm),
        scratch_shapes=[
            pltpu.VMEM((COEFFS, LEAF_DEV), F32),
            pltpu.VMEM((1, COEFFS), F32),
            dma((4,)),
        ],
        compiler_params=pltpu.CompilerParams(vmem_limit_bytes=63 * 1024 * 1024),
    )(*results)


def solution(mesh):
    placed = (
        P(("top", "low"), None, None),
        P(("top", "low"), None),
        P(("top", "low"), None),
        P(("top", "low")),
    )
    return jax.shard_map(
        functools.partial(local, mesh.size, mesh.shape["low"]),
        mesh=mesh,
        in_specs=placed,
        out_specs=(P(None, ("top", "low")), P(("top", "low"), None)),
        check_vma=False,
    )
```

```python
import functools
import math

import jax
import jax.numpy as jnp
import numpy as np
from jax import lax
from jax.experimental import pallas as pl
from jax.experimental.pallas import tpu as pltpu
from jax.sharding import PartitionSpec as P

MONOS = 35
COEFFS = 315
LEAF_DEV = 128
SLOTS = 16
ROWS = 2 * SLOTS + SLOTS // 2
MESH = pl.DeviceIdType.MESH
BF16 = jnp.bfloat16
F32 = jnp.float32
NT = (((1,), (1,)), ((), ()))
NN = (((1,), (0,)), ((), ()))


def make_exponents():
    collected = []
    for degree_total in range(5):
        for first_power in range(degree_total, -1, -1):
            for second_power in range(degree_total - first_power, -1, -1):
                collected.append(
                    (first_power, second_power, degree_total - first_power - second_power)
                )
    return collected


EXPONENTS = make_exponents()
POINTS = (
    (-math.sqrt(0.6), 5.0 / 18.0),
    (0.0, 8.0 / 18.0),
    (math.sqrt(0.6), 5.0 / 18.0),
)


def make_permutation():
    table = np.zeros((320, 384), np.float32)
    for m in range(MONOS):
        for a in range(9):
            table[MONOS * a + m, 128 * (m // 14) + 9 * (m % 14) + a] = 1.0
    return table


def make_shift_tiles(depth, scale):
    tiles, places = [], []
    for target in EXPONENTS:
        table = np.zeros((40, 384), np.float32)
        for n, source in enumerate(EXPONENTS):
            rest = tuple(t - s for t, s in zip(target, source))
            if min(rest) < 0:
                continue
            factor = scale
            for t, s, d in zip(target, source, depth):
                factor *= math.comb(t, s) * 2.0 ** (-d * s)
            lane = 128 * (n // 14) + 9 * (n % 14)
            table[EXPONENTS.index(rest), lane : lane + 9] = factor
        found = []
        for i in range(5):
            for j in range(3):
                tile = table[8 * i : 8 * i + 8, 128 * j : 128 * j + 128]
                if tile.any():
                    found.append((i, j, len(tiles)))
                    tiles.append(tile)
        places.append(found)
    return np.stack(tiles), places


def split(x):
    high = x.astype(BF16)
    low = (x - high.astype(F32)).astype(BF16)
    return high, low


def dot(a, b, dims):
    return lax.dot_general(a, b, dims, preferred_element_type=F32)


def monomials(middle, half):
    total = None
    for point, weight in POINTS:
        at = [m + point * h if point else m for m, h in zip(middle, half)]
        made = {(0, 0, 0): None}
        values = []
        for e in EXPONENTS[1:]:
            axis = next(i for i in range(3) if e[i] > 0)
            lower = tuple(p - (i == axis) for i, p in enumerate(e))
            before = made[lower]
            made[e] = at[axis] * weight if before is None else before * at[axis]
            values.append(made[e])
        total = values if total is None else [x + y for x, y in zip(total, values)]
    return [jnp.ones_like(middle[0])] + total


def pair_products(quads, tensors):
    q_high, q_low = split(jnp.concatenate(quads, axis=0))
    stacked = jnp.concatenate(tensors + [jnp.zeros((56, 128), F32)], axis=0)
    right = jnp.concatenate(split(jnp.transpose(stacked)), axis=1)
    left = jnp.concatenate([q_high, q_low], axis=1)
    both = dot(left, jnp.concatenate([right, right], axis=0), NN)
    return both[:, :128] + both[:, 128:]


def lay_out(pieces, lane):
    tiles = []
    for first in (0, 14, 28):
        tile = jnp.zeros((8, 128), F32)
        for k in reversed(range(min(14, MONOS - first))):
            tile = jnp.where(lane < 9 * k + 9, pieces[first + k], tile)
        tiles.append(tile)
    return tiles


def pick_same(products, index, lane):
    pieces = [
        jnp.take_along_axis(
            products[8 * m : 8 * m + 8], index, axis=1, mode="promise_in_bounds"
        )
        for m in range(MONOS)
    ]
    return lay_out(pieces, lane)


def column(row):
    return jnp.transpose(jnp.broadcast_to(row, (128, 128)))


def kernel(
    devices, low_size, depth, tile_places,
    seg_hbm, leaf_hbm, perm_hbm, spread_hbm, count_hbm, offset_hbm, shift_hbm, power_hbm,
    leaf_out, root_out,
    seg_ref, leaf_ref, perm_ref, spread_ref, count_ref, offset_ref, shift_ref, power_ref,
    place, sbuf, rbuf, root_send, root_recv,
    leaf_made, root_made,
    load_sem, send_sem, recv_sem, root_send_sem, root_recv_sem, out_sem,
):
    blocks = seg_ref.shape[1] - SLOTS
    body_rows = pl.ds(0, blocks)
    fetches = [
        pltpu.make_async_copy(src, dst, load_sem.at[i])
        for i, (src, dst) in enumerate(
            (
                (leaf_hbm, leaf_ref),
                (seg_hbm, seg_ref.at[:, body_rows]),
                (spread_hbm, spread_ref),
                (count_hbm, count_ref),
                (offset_hbm, offset_ref),
                (perm_hbm, perm_ref),
                (shift_hbm, shift_ref),
                (power_hbm, power_ref),
            )
        )
    ]
    for fetch in fetches:
        fetch.start()

    me = lax.axis_index("top") * low_size + lax.axis_index("low")

    def distance(step):
        later = jnp.where(step + 3 >= devices, step + 4 - devices, step + 3)
        return jnp.where(step == 0, 0, later)

    def partner(step):
        other = lax.rem(me + distance(step), devices)
        return other, (other // low_size, lax.rem(other, low_size))

    barrier = pltpu.get_barrier_semaphore()

    def greet(step, carry):
        pl.semaphore_signal(barrier, inc=1, device_id=partner(step)[1], device_id_type=MESH)
        return carry

    lax.fori_loop(1, devices, greet, 0)
    seg_ref[:, blocks:] = jnp.zeros((9, SLOTS, 128), F32)
    place[blocks:] = jnp.zeros((SLOTS, 128), F32)

    fetches[0].wait()
    leaves = leaf_ref[...]
    for chunk in range(blocks // 128):
        place[chunk * 128 : chunk * 128 + 128] = column(
            leaves[chunk : chunk + 1].astype(F32)
        )
    for fetch in fetches[1:5]:
        fetch.wait()

    lane8 = lax.broadcasted_iota(jnp.int32, (8, 128), 1)
    row8 = lax.broadcasted_iota(jnp.int32, (8, 128), 0)
    same = 8 * lax.rem(lane8, 9) + row8

    def load(rows):
        parts = [seg_ref[c, rows, :] for c in range(9)]
        scaled = [h * (2.0 / math.sqrt(128.0)) for h in parts[6:9]]
        tensors = [b * h for b in parts[0:3] for h in scaled]
        return parts[3:6], parts[6:9], tensors

    def block_copy(step):
        return pltpu.make_async_remote_copy(
            src_ref=sbuf.at[step], dst_ref=rbuf.at[step],
            send_sem=send_sem.at[step], recv_sem=recv_sem.at[step],
            device_id=partner(step)[1], device_id_type=MESH,
        )

    def root_copy(step):
        return pltpu.make_async_remote_copy(
            src_ref=root_send, dst_ref=root_recv.at[step],
            send_sem=root_send_sem.at[step], recv_sem=root_recv_sem.at[step],
            device_id=partner(step)[1], device_id_type=MESH,
        )

    pl.semaphore_wait(barrier, devices - 1)

    def send(turn, carry):
        steps, products, leaf_rows = [], [], []
        for u in range(2):
            step = lax.rem(turn * 2 + u + 1, devices)
            owner = partner(step)[0]
            for side in (0, 8):
                rows = pl.ds(offset_ref[0, owner] + side, 8)
                middle, half, tensors = load(rows)
                products.append(pair_products(monomials(middle, half), tensors))
                leaf = jnp.where(row8 + side < count_ref[0, owner], place[rows, :], -1.0)
                leaf_rows.append(leaf)
            steps.append(step)
        made = [pick_same(one, same, lane8) for one in products]
        for u, step in enumerate(steps):
            near, far = made[2 * u : 2 * u + 2]
            last_near = jnp.where(lane8 == 63, leaf_rows[2 * u], near[2])
            last_far = jnp.where(lane8 == 63, leaf_rows[2 * u + 1], far[2])
            sbuf[step, 0:8, :] = near[0]
            sbuf[step, 8:16, :] = far[0]
            sbuf[step, 16:24, :] = near[1]
            sbuf[step, 24:32, :] = far[1]
            sbuf[step, 32:40, :] = jnp.where(lane8 < 64, last_near, pltpu.roll(last_far, 64, 1))

            @pl.when(step != 0)
            def _():
                block_copy(step).start()

        return carry

    lax.fori_loop(0, devices // 2, send, 0)
    rbuf[0] = sbuf[0]

    def unfold(ref, start, end):
        rows = (end - start) * 8
        got = [ref[start:end, at : at + 8].reshape(rows, 128) for at in range(0, ROWS, 8)]
        return got[0::2], [got[1], got[3], pltpu.roll(got[4], 64, 1)]

    fetches[6].wait()
    fetches[7].wait()
    rows = devices * 8
    shape = (rows, 128)
    steps = lax.shift_right_logical(lax.broadcasted_iota(jnp.int32, shape, 0), 3)
    owner = me + distance(steps)
    owner = jnp.where(owner >= devices, owner - devices, owner)
    powers = [power_ref[d : d + 1, :] for d in range(3)]
    lane_used = lax.broadcasted_iota(jnp.int32, shape, 1) < MONOS
    grown = jnp.zeros((128, 384), F32)
    for side in unfold(sbuf, 0, devices):
        leaf = jnp.broadcast_to(side[2][:, 63:64], shape)
        cell = owner * LEAF_DEV + leaf.astype(jnp.int32)
        factor = jnp.where((leaf >= 0.0) & lane_used, 1.0, 0.0)
        for d in range(3):
            bits = jnp.zeros(shape, jnp.int32)
            for j in range(depth[d]):
                moved = lax.shift_right_logical(cell, 2 * j + d) if 2 * j + d else cell
                bits = bits | (moved & (1 << j))
            centre = bits.astype(F32) * 2.0 ** (1 - depth[d]) - (1.0 - 2.0 ** -depth[d])
            for least in range(1, 5):
                factor = factor * jnp.where(powers[d] >= least, centre, 1.0)
        c_high, c_low = split(jnp.transpose(factor))
        high, low = split(jnp.concatenate(side, axis=1))
        grown = grown + dot(c_high, high, NN) + dot(c_low, high, NN) + dot(c_high, low, NN)
    sums = []
    for found in tile_places:
        total = None
        for i, j, at in found:
            term = grown[8 * i : 8 * i + 8, 128 * j : 128 * j + 128] * shift_ref[at]
            total = term if total is None else total + term
        sums.append(total)
    sums = jnp.concatenate(split(jnp.concatenate(sums, axis=0)), axis=1)
    sums = dot(sums, spread_ref[...], NN)
    tiles = lay_out([sums[8 * m : 8 * m + 8] for m in range(MONOS)], lane8)
    own = jnp.concatenate(
        [jnp.sum(t, axis=0, keepdims=True) for t in tiles] + [jnp.zeros((1, 128), F32)], axis=0
    )
    root_send[...] = own

    def send_root(step, carry):
        root_copy(step).start()
        return carry

    lax.fori_loop(1, devices, send_root, 0)

    def take(step, carry):
        block_copy(step).wait()
        return carry

    cells = jnp.zeros((LEAF_DEV, 384), F32)
    bounds = [0, devices // 2, devices // 8 * 7, devices]
    for start, end in zip(bounds[:-1], bounds[1:]):
        lax.fori_loop(max(start, 1), end, take, 0)
        rows = (end - start) * 8
        leaf_lane = lax.broadcasted_iota(jnp.int32, (rows, 128), 1).astype(F32)
        for side in unfold(rbuf, start, end):
            hit = jnp.where(side[2][:, 63:64] == leaf_lane, 1.0, 0.0)
            hit = jnp.transpose(hit).astype(BF16)
            high, low = split(jnp.concatenate(side, axis=1))
            cells = cells + dot(hit, high, NN) + dot(hit, low, NN)
    fetches[5].wait()
    perm = perm_ref[...]
    high, low = split(cells)
    leaf_made[...] = (dot(perm, high, NT) + dot(perm, low, NT))[:COEFFS]
    leaf_store = pltpu.make_async_copy(leaf_made, leaf_out, out_sem.at[0])
    leaf_store.start()

    def take_root(step, carry):
        root_copy(step).wait()
        return carry

    lax.fori_loop(1, devices, take_root, 0)
    root_recv[0] = own
    total = jnp.sum(root_recv[...], axis=0)
    line = jnp.concatenate([total[0:1], total[1:2], total[2:3]], axis=1)
    high, low = split(jnp.broadcast_to(line, (16, 384)))
    root_made[...] = (dot(high, perm, NT) + dot(low, perm, NT))[0:1, :COEFFS]
    root_store = pltpu.make_async_copy(root_made, root_out, out_sem.at[1])
    root_store.start()
    leaf_store.wait()
    root_store.wait()


def hand_over(leaf_in, root_in, leaf_out, root_out, leaf_held, root_held, sem):
    incoming = [
        pltpu.make_async_copy(leaf_in, leaf_held, sem.at[0]),
        pltpu.make_async_copy(root_in, root_held, sem.at[1]),
    ]
    outgoing = [
        pltpu.make_async_copy(leaf_held, leaf_out, sem.at[2]),
        pltpu.make_async_copy(root_held, root_out, sem.at[3]),
    ]
    for copy in incoming:
        copy.start()
    for first, then in zip(incoming, outgoing):
        first.wait()
        then.start()
    for copy in outgoing:
        copy.wait()


def local(devices, low_size, segments, send_counts, send_offsets, leaf_of_block):
    blocks = segments.shape[0]
    levels = LEAF_DEV.bit_length() - 1 + devices.bit_length() - 1
    depth = [len(range(d, levels, 3)) for d in range(3)]
    shift_tiles, tile_places = make_shift_tiles(depth, 2.0 ** (-levels / 2))
    powers = np.zeros((8, 128), np.int32)
    powers[:3, :MONOS] = np.array(EXPONENTS).T
    lanes = np.arange(128)
    spread = (lanes[None, :] % 9 == lanes[:, None] % 9) & (lanes[:, None] < 126)
    spread = np.concatenate([spread, spread], axis=0).astype(np.float32)
    spread = jnp.asarray(spread, BF16)
    perm = jnp.asarray(make_permutation(), BF16)
    hbm = pl.BlockSpec(memory_space=pltpu.HBM)
    dma = pltpu.SemaphoreType.DMA
    shapes = (
        jax.ShapeDtypeStruct((COEFFS, LEAF_DEV), F32),
        jax.ShapeDtypeStruct((1, COEFFS), F32),
    )
    results = pl.pallas_call(
        functools.partial(kernel, devices, low_size, depth, tile_places),
        out_shape=shapes,
        in_specs=[hbm] * 8,
        out_specs=(hbm, hbm),
        scratch_shapes=[
            pltpu.VMEM((9, blocks + SLOTS, 128), F32),
            pltpu.VMEM((blocks // 128, 128), jnp.int32),
            pltpu.VMEM((320, 384), BF16),
            pltpu.VMEM((256, 128), BF16),
            pltpu.SMEM((1, devices), jnp.int32),
            pltpu.SMEM((1, devices), jnp.int32),
            pltpu.VMEM(shift_tiles.shape, F32),
            pltpu.VMEM(powers.shape, jnp.int32),
            pltpu.VMEM((blocks + SLOTS, 128), F32),
            pltpu.VMEM((devices, ROWS, 128), F32),
            pltpu.VMEM((devices, ROWS, 128), F32),
            pltpu.VMEM((4, 128), F32),
            pltpu.VMEM((devices, 4, 128), F32),
            pltpu.VMEM((COEFFS, LEAF_DEV), F32),
            pltpu.VMEM((1, COEFFS), F32),
            dma((8,)),
            dma((devices,)),
            dma((devices,)),
            dma((devices,)),
            dma((devices,)),
            dma((2,)),
        ],
        compiler_params=pltpu.CompilerParams(
            collective_id=0, has_side_effects=True, vmem_limit_bytes=63 * 1024 * 1024
        ),
        cost_estimate=pl.CostEstimate(
            flops=2 * blocks * 128 * COEFFS * 2, bytes_accessed=blocks * 128 * 40, transcendentals=0
        ),
    )(
        jnp.transpose(segments, (1, 0, 2)),
        leaf_of_block.reshape(blocks // 128, 128),
        perm,
        spread,
        send_counts,
        send_offsets,
        jnp.asarray(shift_tiles),
        jnp.asarray(powers),
    )
    return pl.pallas_call(
        hand_over,
        out_shape=shapes,
        in_specs=[hbm, hbm],
        out_specs=(hbm, hbm),
        scratch_shapes=[
            pltpu.VMEM((COEFFS, LEAF_DEV), F32),
            pltpu.VMEM((1, COEFFS), F32),
            dma((4,)),
        ],
        compiler_params=pltpu.CompilerParams(vmem_limit_bytes=63 * 1024 * 1024),
    )(*results)


def solution(mesh):
    placed = (
        P(("top", "low"), None, None),
        P(("top", "low"), None),
        P(("top", "low"), None),
        P(("top", "low")),
    )
    return jax.shard_map(
        functools.partial(local, mesh.size, mesh.shape["low"]),
        mesh=mesh,
        in_specs=placed,
        out_specs=(P(None, ("top", "low")), P(("top", "low"), None)),
        check_vma=False,
    )
```
